32 devices in a mesh: groups: 1, frame: 4 (over y, x), row: 8 (over z, core).
Axes of the slice: x: 2, y: 2, z: 4, core: 2. Of those that a mesh axis runs over, the one named last changes fastest.
Arguments:
- layer_input: bfloat16 [4096, 3072], P(('groups', 'frame', 'row')), may hold values from -6 to 6
- queries: bfloat16 [4096, 3072], P(('groups', 'frame', 'row')), may hold values from -64 to 64
- key_input: bfloat16 [4096, 3072], P(('groups', 'frame', 'row')), may hold values from -4.5 to 4.5
- values: bfloat16 [4096, 3072], P(('groups', 'frame', 'row')), may hold values from -6 to 6
- key_tiles: int32 [32, 5], P(('groups', 'frame', 'row')), may hold values from -1 to 31, as said below
- expert_ids: int32 [4096, 2], P(('groups', 'frame', 'row')), may hold values from 0 to 3, all different within a row; in each aligned block of 128 rows (0 to 127, 128 to 255, ...) at most 128 rows name the same one
- norm_gain: float32 [3072], replicated, may hold values from 0.5 to 1.5
- router: bfloat16 [3072, 4], replicated, may hold values from -0.109375 to 0.109375
- w_up: bfloat16 [8, 3072, 768], P('row'), may hold values from -0.109375 to 0.109375
- w_down: bfloat16 [8, 768, 3072], P('row'), may hold values from -0.15625 to 0.15625
Outputs:
- layer_output: bfloat16 [4096, 3072], P(('groups', 'frame', 'row'))
The draws below stay inside these ranges and needn't reach their ends.
Inputs may be any that keep to these rules, and one draw needn't show every extreme that they name: `key_tiles`: entry 0 of row t is t. Then come, in any order, distinct tiles among the up to four whose frame position or row position differs from t's by one while the other is the same; the remaining entries are -1. Some tile lists all four. `expert_ids`: each row names two different experts. Within the rows of one device no expert is named more than 128 times, and in every draw some expert is named exactly 128 times there.
All inputs are finite; a program needn't handle non-finite values.
Results may differ from the reference program's by a relative error of at most 0.007.
Values may be sent and summed in bfloat16 or wider, within the bound.
A program may use at most 128 MiB of HBM per device.

```python
import math
import jax
import jax.numpy as jnp
import numpy as np
from jax import lax

D = 3072
HEADS = 24
FF = 1536
FF_HALF = 768
TILE = 128
TOK_DEV = 128
ROW_TILES = 8
TILES = 32
TOKENS = 4096
EXPERTS = 4
CAP = 128
N_FRAME = 4
N_ROW = 8


def base_field(key):
    return jax.random.normal(key, (TOKENS, D), jnp.float32)


def draw_key_input(key, part):
    field = base_field(key)
    return jnp.clip(field, -4.5, 4.5).astype(jnp.bfloat16)


def draw_queries(key, part):
    key = jax.random.fold_in(key, 5)
    fresh = jax.random.normal(key, (TOKENS, D), jnp.float32)
    return jnp.clip(fresh, -4.5, 4.5).astype(jnp.bfloat16)


def draw_key_tiles(key, part):
    key = jax.random.fold_in(key, 11)
    coin_key = jax.random.fold_in(key, 1)
    order_key = jax.random.fold_in(key, 2)
    tile_ids = jnp.arange(TILES, dtype=jnp.int32)
    frame_pos = tile_ids // ROW_TILES
    row_pos = tile_ids % ROW_TILES
    frame_step = jnp.array([-1, 1, 0, 0], jnp.int32)
    row_step = jnp.array([0, 0, -1, 1], jnp.int32)
    near_frame = frame_pos[:, None] + frame_step[None, :]
    near_row = row_pos[:, None] + row_step[None, :]
    inside = (near_frame >= 0) & (near_frame < N_FRAME) & (near_row >= 0) & (near_row < ROW_TILES)
    coins = jax.random.randint(coin_key, (TILES, 4), 0, 2)
    forced = ((frame_pos == 1) & (row_pos % 3 == 1) & (row_pos < ROW_TILES - 1))[:, None]
    keep = inside & ((coins == 1) | forced)
    neighbour_ids = near_frame * ROW_TILES + near_row
    ranks = jax.random.randint(order_key, (TILES, 4), 0, 1024) * 4 + jnp.arange(4, dtype=jnp.int32)[None, :]
    scores = jnp.where(keep, ranks, 8192 + jnp.arange(4, dtype=jnp.int32)[None, :])
    order = jnp.argsort(scores, axis=1)
    picked = jnp.take_along_axis(jnp.where(keep, neighbour_ids, -1), order, axis=1)
    return jnp.concatenate([tile_ids[:, None], picked], axis=1).astype(jnp.int32)


def levels(stream_key, shape, shards, low, largest):
    def one(dim, shards_of):
        heights = jax.random.uniform(jax.random.fold_in(jax.random.fold_in(stream_key, 6), dim), (shards_of,), jnp.float32, low / len(shards), largest / len(shards))
        return jnp.repeat(jnp.exp(heights), shape[dim] // shards_of).reshape((-1,) + (1,) * (len(shape) - dim - 1))

    level = one(*shards[0])
    for cut in shards[1:]:
        level = level * one(*cut)
    return level


def assign_block(stream_key, own, number, rows, number_of, top, limit, slope):
    sequence = jax.random.permutation(stream_key, number_of)
    crowded, ordinary = load_shares(number_of, rows * top, limit, slope, True), load_shares(number_of, rows * top, limit, slope, False)
    places = jnp.arange(number_of)

    def named(lengths, rotation):
        used = int((lengths > 0).sum())
        fixed = max(1, used // 4)
        moved = fixed + (places - fixed + rotation * (used - fixed)) % max(1, number_of - fixed)
        return jnp.zeros((number_of,), jnp.int32).at[sequence[jnp.where(places < fixed, places, moved)]].set(jnp.asarray(lengths, jnp.int32))

    lengths = jnp.where(number % 4 == 0, named(crowded, number // 4), named(ordinary, number - number // 4 - 1))
    mixed = jax.random.permutation(jax.random.fold_in(own, 3), number_of)
    donor, sink = mixed[0:number_of // 2 * 2:2], mixed[1:number_of // 2 * 2:2]
    slack = jnp.minimum(lengths[donor] - 1, limit - lengths[sink]) // 2
    slack = jnp.where((donor == sequence[0]) | (sink == sequence[0]) | (lengths[sink] == 0), 0, jnp.maximum(slack, 0))
    moved = jax.random.randint(jax.random.fold_in(own, 4), (number_of // 2,), 0, 1 << 20) % (slack + 1)
    lengths = lengths.at[donor].add(-moved).at[sink].add(moved)
    items = jnp.searchsorted(jnp.cumsum(lengths), jnp.arange(rows * top), side="right").astype(jnp.int32)
    table = items.reshape(top, rows).T
    table = table[jax.random.permutation(jax.random.fold_in(own, 1), rows)]
    rotation = jax.random.randint(jax.random.fold_in(own, 2), (rows, 1), 0, top)
    return jnp.take_along_axis(table, (jnp.arange(top)[None, :] + rotation) % top, axis=1)


def load_shares(count, total, reach, skew, full):
    portions = [(1 << 20) // math.isqrt(grade ** skew) + 1 for grade in range(1, count + 1)]
    largest = reach if full else min(reach, max(-(-total // count), total * portions[0] // sum(portions)))
    least = 1 if total - largest >= count - 1 else 0
    given, surplus = [largest] + [least] * (count - 1), total - largest - least * (count - 1)
    while surplus > 0:
        free = [i for i in range(1, count) if given[i] < largest] or [i for i in range(1, count) if given[i] < reach]
        whole, left = sum([portions[i] for i in free]), surplus
        for i in free:
            addition = min(reach - given[i], max(1, left * portions[i] // whole), surplus)
            given[i] = given[i] + addition
            surplus = surplus - addition
    return np.array(given)


def normal_values(stream_key, dims, deviation, most, shards=(), kind=jnp.bfloat16):
    entries = deviation * jax.random.normal(stream_key, dims, jnp.float32)
    if shards:
        entries = entries * levels(stream_key, dims, shards, -0.22, 0.18)
    return jnp.clip(entries, -most, most).astype(kind)


def setup_inputs(seed: int = 0, part: int = 0) -> dict:
    splits = jax.random.split(jax.random.key(seed), 11)
    part_splits = jax.random.split(jax.random.fold_in(splits[10], part), 11)
    layer_input = normal_values(part_splits[0], (TOKENS, D), 1.0, 6.0, ((0, 32),))
    queries = draw_queries(jax.random.fold_in(jax.random.fold_in(splits[10], part), 71), part)
    key_input = draw_key_input(jax.random.fold_in(jax.random.fold_in(splits[10], part), 71), part)
    values = normal_values(part_splits[3], (TOKENS, D), 1.0, 6.0, ((0, 32),))
    key_tiles = draw_key_tiles(jax.random.fold_in(jax.random.fold_in(splits[10], part), 71), part)
    expert_ids_keys = jax.random.split(jax.random.fold_in(part_splits[5], 1), TOKENS // TOK_DEV)
    expert_ids_turns = jax.random.permutation(jax.random.fold_in(part_splits[5], 3), TOKENS // TOK_DEV)
    expert_ids = jax.vmap(lambda own, number: assign_block(jax.random.fold_in(part_splits[5], 2), own, number, TOK_DEV, EXPERTS, 2, CAP, 1))(expert_ids_keys, expert_ids_turns).reshape((TOKENS, 2))
    norm_gain = jnp.clip(1.0 + 0.1 * jax.random.normal(splits[6], (D,), jnp.float32), 0.5, 1.5)
    router = normal_values(splits[7], (D, EXPERTS), D ** -0.5, 0.109375)
    w_up = normal_values(splits[8], (2 * EXPERTS, D, FF_HALF), D ** -0.5, 0.109375, ((0, 8),))
    w_down = normal_values(splits[9], (2 * EXPERTS, FF_HALF, D), FF ** -0.5, 0.15625, ((0, 8),))
    return dict(layer_input=layer_input, queries=queries, key_input=key_input, values=values, key_tiles=key_tiles, expert_ids=expert_ids, norm_gain=norm_gain, router=router, w_up=w_up, w_down=w_down)


def tile_partials(query_rows, key_rows, value_rows, head_count):
    batches, row_count, features = query_rows.shape
    head_size = features // head_count
    query_split = query_rows.astype(jnp.float32).reshape(batches, row_count, head_count, head_size)
    key_split = key_rows.astype(jnp.float32).reshape(batches, -1, head_count, head_size)
    value_split = value_rows.astype(jnp.float32).reshape(batches, -1, head_count, head_size)
    scores = jnp.einsum('bqhd,bkhd->bhqk', query_split, key_split) * head_size ** (-0.5)
    maxima = lax.optimization_barrier(jnp.max(scores, axis=-1))
    expos = jnp.exp(scores - maxima[..., None])
    totals = lax.optimization_barrier(jnp.sum(expos, axis=-1))
    probs = lax.optimization_barrier(expos.astype(jnp.bfloat16)).astype(jnp.float32)
    mixed = jnp.einsum('bhqk,bkhd->bqhd', probs, value_split)
    mixed = mixed / jnp.transpose(totals, (0, 2, 1))[..., None]
    return (mixed.reshape(batches, row_count, features).astype(jnp.bfloat16), maxima, totals)

def merge_partials(partial_value, maxima, totals, listed, head_count):
    masked = jnp.where(listed[:, :, None, None], maxima, -jnp.inf)
    peak_value = lax.optimization_barrier(jnp.max(masked, axis=1, keepdims=True))
    weights = totals * jnp.exp(masked - peak_value)
    weight_sum = lax.optimization_barrier(jnp.sum(weights, axis=1))
    tiles_here, cands, row_count, features = partial_value.shape
    split = partial_value.astype(jnp.float32).reshape(tiles_here, cands, row_count, head_count, features // head_count)
    scaled = lax.optimization_barrier(jnp.sum(split * jnp.transpose(weights, (0, 1, 3, 2))[..., None], axis=1))
    merged = scaled / jnp.transpose(weight_sum, (0, 2, 1))[..., None]
    return merged.reshape(tiles_here, row_count, features)

def reference(layer_input, queries, key_input, values, key_tiles, expert_ids, norm_gain, router, w_up, w_down):
    query_stack = queries.reshape(TILES, TILE, D)
    key_stack = key_input.reshape(TILES, TILE, D)
    value_stack = values.reshape(TILES, TILE, D)

    def one_tile(packed):
        query_block, listing = packed
        usable = listing >= 0
        chosen = jnp.where(usable, listing, 0).astype(jnp.int32)
        key_block = key_stack[chosen]
        value_block = value_stack[chosen]
        repeated = jnp.broadcast_to(query_block[None], key_block.shape)
        partial_value, maxima, totals = tile_partials(repeated, key_block, value_block, HEADS)
        return merge_partials(partial_value[None], maxima[None], totals[None], usable[None], HEADS)[0]
    attended = lax.map(one_tile, (query_stack, key_tiles))
    hidden_state = layer_input.astype(jnp.float32) + attended.reshape(TOKENS, D)
    mean_square = lax.optimization_barrier(jnp.mean(hidden_state * hidden_state, axis=1, keepdims=True))
    normed = (hidden_state * lax.rsqrt(mean_square + 1e-06) * norm_gain).astype(jnp.bfloat16)
    logits = jnp.dot(normed, router, preferred_element_type=jnp.float32)
    gates = jax.nn.sigmoid(jnp.take_along_axis(logits, expert_ids, axis=1))
    device_count = N_FRAME * N_ROW
    block_ids = expert_ids.reshape(device_count, TOK_DEV * 2)
    onehot = (block_ids[:, :, None] == jnp.arange(EXPERTS, dtype=jnp.int32)[None, None, :]).astype(jnp.int32)
    earlier = jnp.cumsum(onehot, axis=1) - onehot
    slot_index = lax.optimization_barrier(jnp.sum(earlier * onehot, axis=2)).astype(jnp.int32)
    owner_base = (jnp.arange(device_count, dtype=jnp.int32) * CAP)[:, None]
    position = (slot_index + owner_base).reshape(-1).astype(jnp.int32)
    flat_ids = expert_ids.reshape(-1)
    flat_gates = gates.reshape(-1)
    doubled = jnp.repeat(normed, 2, axis=0)
    slot_limit = device_count * CAP

    def per_expert(running, expert):
        chosen = flat_ids == expert
        where_to = jnp.where(chosen, position, slot_limit).astype(jnp.int32)
        sectioned = jnp.zeros((slot_limit, D), jnp.bfloat16).at[where_to].set(doubled, mode='drop')
        combined = jnp.zeros((slot_limit, D), jnp.float32)
        for half in range(2):
            up_part = jnp.dot(sectioned, w_up[2 * expert + half], preferred_element_type=jnp.float32)
            inner = jax.nn.gelu(up_part, approximate=True).astype(jnp.bfloat16)
            result = jnp.dot(inner, w_down[2 * expert + half], preferred_element_type=jnp.float32)
            combined = combined + lax.optimization_barrier(result.astype(jnp.bfloat16)).astype(jnp.float32)
        fetched = combined[jnp.minimum(where_to, slot_limit - 1)]
        term = jnp.where(chosen[:, None], flat_gates[:, None] * fetched, jnp.zeros_like(fetched))
        return (running + lax.optimization_barrier(jnp.sum(term.reshape(TOKENS, 2, D), axis=1)), None)
    total, _ = lax.scan(per_expert, hidden_state, jnp.arange(EXPERTS, dtype=jnp.int32))
    return total.astype(jnp.bfloat16)
```

```python
import functools

import jax
import jax.numpy as jnp
from jax import lax
from jax.experimental import pallas as pl
from jax.experimental.pallas import tpu as pltpu
from jax.sharding import PartitionSpec as P

HEADS = 24
TILE = 128


def shifted(value, axis, steps):
    count = lax.axis_size(axis)
    initial, last = (max(0, -steps), min(count, count - steps))
    return lax.ppermute(value, axis, [(source, source + steps) for source in range(initial, last)])


def with_halo(block, sides, width):
    for axis, dim in sides:
        count = lax.axis_size(axis)
        forward = [(i, i + 1) for i in range(count - 1)]
        backward = [(target, source) for source, target in forward]
        low = lax.ppermute(
            lax.slice_in_dim(block, block.shape[dim] - width, None, axis=dim), axis, forward
        )
        high = lax.ppermute(lax.slice_in_dim(block, 0, width, axis=dim), axis, backward)
        block = jnp.concatenate([low, block, high], axis=dim)
    return block


def tile_partials(query_rows, key_rows, value_rows, head_count):
    batches, row_count, features = query_rows.shape
    head_size = features // head_count
    query_split = query_rows.reshape(batches, row_count, head_count, head_size)
    key_split = key_rows.reshape(batches, -1, head_count, head_size)
    value_split = value_rows.reshape(batches, -1, head_count, head_size)
    scores = jnp.einsum(
        "bqhd,bkhd->bhqk", query_split, key_split, preferred_element_type=jnp.float32
    ) * head_size ** (-0.5)
    maxima = jnp.max(scores, axis=-1)
    expos = jnp.exp(scores - maxima[..., None])
    totals = jnp.sum(expos, axis=-1)
    mixed = jnp.einsum(
        "bhqk,bkhd->bqhd",
        expos.astype(jnp.bfloat16),
        value_split,
        preferred_element_type=jnp.float32,
    )
    mixed = mixed / jnp.transpose(totals, (0, 2, 1))[..., None]
    return (mixed.reshape(batches, row_count, features).astype(jnp.bfloat16), maxima, totals)


def merge_partials(partial_value, maxima, totals, listed, head_count):
    masked = jnp.where(listed[:, :, None, None], maxima, -jnp.inf)
    peak_value = jnp.max(masked, axis=1, keepdims=True)
    weights = totals * jnp.exp(masked - peak_value)
    weight_sum = jnp.sum(weights, axis=1)
    tiles_here, cands, row_count, features = partial_value.shape
    split = partial_value.reshape(tiles_here, cands, row_count, head_count, features // head_count)
    scaled = jnp.sum(split * jnp.transpose(weights, (0, 1, 3, 2))[..., None], axis=1)
    merged = scaled / jnp.transpose(weight_sum, (0, 2, 1))[..., None]
    return merged.reshape(tiles_here, row_count, features)


def frame_return(part_out, part_max, part_sum, offset):
    return (
        shifted(part_out.astype(jnp.float32), "frame", offset).astype(part_out.dtype),
        shifted(part_max, "frame", offset),
        shifted(part_sum, "frame", offset),
    )


def row_return(part_out, part_max, part_sum, offset):
    return (
        shifted(part_out.astype(jnp.float32), "row", offset).astype(part_out.dtype),
        shifted(part_max, "row", offset),
        shifted(part_sum, "row", offset),
    )


def half_expert(token_rows, w_up, w_down):
    up_part = jnp.dot(token_rows, w_up[0], preferred_element_type=jnp.float32)
    inner = jax.nn.gelu(up_part, approximate=True).astype(jnp.bfloat16)
    return jnp.dot(inner, w_down[0], preferred_element_type=jnp.float32).astype(jnp.bfloat16)


def plain(
    layer_input, queries, key_input, values, key_tiles, expert_ids, norm_gain, router, w_up, w_down
):
    head_count = HEADS
    tile_rows = TILE
    per_device = key_tiles.shape[0]
    features = layer_input.shape[1]
    frame_index = lax.axis_index("frame")
    row_index = lax.axis_index("row")
    frame_count = lax.axis_size("frame")
    row_count = lax.axis_size("row")
    row_tiles = row_count * per_device
    query_tiles = queries.reshape(per_device, tile_rows, features)
    extended = with_halo(query_tiles[None], (("frame", 0), ("row", 1)), 1)
    middle = extended[1]
    visitors = jnp.stack(
        [
            query_tiles,
            extended[0, 1 : per_device + 1],
            extended[2, 1 : per_device + 1],
            middle[0:per_device],
            middle[2 : per_device + 2],
        ]
    )
    own_keys = jnp.broadcast_to(
        key_input.reshape(1, per_device, tile_rows, features), (5, per_device, tile_rows, features)
    )
    own_values = jnp.broadcast_to(
        values.reshape(1, per_device, tile_rows, features), (5, per_device, tile_rows, features)
    )
    flat_shape = (5 * per_device, tile_rows, features)
    partial_value, maxima, totals = tile_partials(
        visitors.reshape(flat_shape),
        own_keys.reshape(flat_shape),
        own_values.reshape(flat_shape),
        head_count,
    )
    partial_value = partial_value.reshape(5, per_device, tile_rows, features)
    maxima = maxima.reshape(5, per_device, head_count, tile_rows)
    totals = totals.reshape(5, per_device, head_count, tile_rows)
    from_lower = frame_return(partial_value[2], maxima[2], totals[2], 1)
    from_upper = frame_return(partial_value[1], maxima[1], totals[1], -1)
    below_edge = row_return(partial_value[4], maxima[4], totals[4], 1)
    above_edge = row_return(partial_value[3], maxima[3], totals[3], -1)
    local_sets = (partial_value, maxima, totals)
    from_below = tuple(
        (
            jnp.concatenate([below_edge[member], local_sets[member][4][: per_device - 1]], axis=0)
            for member in range(3)
        )
    )
    from_above = tuple(
        (
            jnp.concatenate([local_sets[member][3][1:], above_edge[member]], axis=0)
            for member in range(3)
        )
    )
    pieces = [
        (partial_value[0], maxima[0], totals[0]),
        from_lower,
        from_upper,
        from_below,
        from_above,
    ]
    partial_value = jnp.stack([piece[0].astype(jnp.float32) for piece in pieces], axis=1)
    maxima = jnp.stack([piece[1] for piece in pieces], axis=1)
    totals = jnp.stack([piece[2] for piece in pieces], axis=1)
    local_tiles = jnp.arange(per_device, dtype=jnp.int32)
    row_pos = row_index * per_device + local_tiles
    tile_id = frame_index * row_tiles + row_pos
    cand_ids = jnp.stack(
        [tile_id, tile_id - row_tiles, tile_id + row_tiles, tile_id - 1, tile_id + 1], axis=1
    )
    inside = jnp.stack(
        [
            jnp.ones((per_device,), bool),
            jnp.broadcast_to(frame_index >= 1, (per_device,)),
            jnp.broadcast_to(frame_index < frame_count - 1, (per_device,)),
            row_pos >= 1,
            row_pos < row_tiles - 1,
        ],
        axis=1,
    )
    listed = inside & jnp.any(key_tiles[:, :, None] == cand_ids[:, None, :], axis=1)
    attended = merge_partials(partial_value, maxima, totals, listed, head_count)
    hidden_state = layer_input.astype(jnp.float32) + attended.reshape(-1, features)
    mean_square = jnp.mean(hidden_state * hidden_state, axis=1, keepdims=True)
    normed = (hidden_state * lax.rsqrt(mean_square + 1e-06) * norm_gain).astype(jnp.bfloat16)
    logits = jnp.dot(normed, router, preferred_element_type=jnp.float32)
    token_count = normed.shape[0]
    expert_count = router.shape[1]
    capacity = min(token_count, max(2, 4 * token_count // expert_count))
    expert_range = jnp.arange(expert_count, dtype=jnp.int32)
    selector = expert_ids[:, :, None] == expert_range[None, None, :]
    gates = jax.nn.sigmoid(jnp.sum(logits[:, None, :] * selector.astype(jnp.float32), axis=2))
    onehot = selector.astype(jnp.int32).reshape(token_count * 2, expert_count)
    earlier = jnp.cumsum(onehot, axis=0) - onehot
    slot_index = jnp.sum(earlier * onehot, axis=1)
    flat_ids = expert_ids.reshape(-1)
    doubled = jnp.repeat(normed, 2, axis=0)
    outgoing = (
        jnp.zeros((expert_count, capacity, features), jnp.bfloat16)
        .at[flat_ids, slot_index]
        .set(doubled)
    )
    padded_out = jnp.repeat(outgoing, 2, axis=0)
    arrived = lax.all_to_all(padded_out, "row", split_axis=0, concat_axis=0, tiled=True)
    result = half_expert(arrived.reshape(-1, features), w_up, w_down)
    returned = lax.all_to_all(
        result.reshape(arrived.shape), "row", split_axis=0, concat_axis=0, tiled=True
    )
    halves = returned.reshape(expert_count, 2, capacity, features)
    both = halves[:, 0].astype(jnp.float32) + halves[:, 1].astype(jnp.float32)
    picked = both[flat_ids, slot_index].reshape(token_count, 2, features)
    return (hidden_state + jnp.sum(gates[:, :, None] * picked, axis=1)).astype(jnp.bfloat16)


HALO_PARTS = 4
SUM_PARTS = 4
MESH = pl.DeviceIdType.MESH


def fused_kernel(
    frames, rows, heads,
    li, q, k, v, bias, gain, router, sel, wup_hbm, wdn_hbm,
    out,
    kb, vb, hid, g, p, sib, fd, fu, hmid, wup, wdn,
    wsem, hsend, hrecv, agu, agd, ags, agr, pss, psr, ups, dns, upr, dnr,
):
    chips = rows // 2
    features = q.shape[1]
    f = lax.axis_index("frame")
    r = lax.axis_index("row")
    z = r // 2
    c = r % 2
    sibling = {"row": 2 * z + 1 - c}
    above = {"row": r + 2}
    below = {"row": r - 2}
    has_above = z < chips - 1
    has_below = z > 0
    sides = (
        (f > 0, {"frame": f - 1}, 1),
        (f < frames - 1, {"frame": f + 1}, 0),
        (r > 0, {"row": r - 1}, 3),
        (r < rows - 1, {"row": r + 1}, 2),
    )

    load_up = pltpu.make_async_copy(wup_hbm.at[0], wup, wsem.at[0])
    load_dn = pltpu.make_async_copy(wdn_hbm.at[0], wdn, wsem.at[1])
    load_up.start()
    load_dn.start()

    barrier = pltpu.get_barrier_semaphore()
    partners = sides + ((has_below, below, 0), (has_above, above, 0))
    for there, who, _ in partners:
        @pl.when(there)
        def _():
            pl.semaphore_signal(barrier, inc=1, device_id=who, device_id_type=MESH)
    peers = sum(jnp.where(there, 1, 0) for there, _, _ in partners)
    pl.semaphore_wait(barrier, peers)

    width = features // HALO_PARTS

    def halo(side, part, which):
        _, who, slot = sides[side]
        cols = pl.ds(part * width, width)
        src, dst = ((k, kb), (v, vb))[which]
        return pltpu.make_async_remote_copy(
            src_ref=src.at[:, cols],
            dst_ref=dst.at[slot, :, cols],
            send_sem=hsend.at[side, part, which],
            recv_sem=hrecv.at[slot, part, which],
            device_id=who,
            device_id_type=MESH,
        )

    def halo_arrival(slot, part, which):
        cols = pl.ds(part * width, width)
        src, dst = ((k, kb), (v, vb))[which]
        return pltpu.make_async_remote_copy(
            src_ref=src.at[:, cols],
            dst_ref=dst.at[slot, :, cols],
            send_sem=hsend.at[slot, part, which],
            recv_sem=hrecv.at[slot, part, which],
            device_id=sides[slot][1],
            device_id_type=MESH,
        )

    for part in range(HALO_PARTS):
        for side in range(4):
            @pl.when(sides[side][0])
            def _():
                halo(side, part, 0).start()
                halo(side, part, 1).start()
    for slot in range(4):
        @pl.when(jnp.logical_not(sides[slot][0]))
        def _():
            kb[slot] = jnp.zeros(kb.shape[1:], kb.dtype)
            vb[slot] = jnp.zeros(vb.shape[1:], vb.dtype)

    scale = TILE ** -0.5
    per_part = heads // HALO_PARTS
    for part in range(HALO_PARTS):
        for slot in range(4):
            @pl.when(sides[slot][0])
            def _():
                halo_arrival(slot, part, 0).wait_recv()
                halo_arrival(slot, part, 1).wait_recv()

        def one_head(h):
            cols = pl.ds(pl.multiple_of(h * TILE, TILE), TILE)
            keys = jnp.concatenate([k[:, cols]] + [kb[s, :, cols] for s in range(4)], axis=0)
            vals = jnp.concatenate([v[:, cols]] + [vb[s, :, cols] for s in range(4)], axis=0)
            scores = lax.dot_general(
                q[:, cols], keys, (((1,), (1,)), ((), ())), preferred_element_type=jnp.float32
            ) * scale + bias[...]
            peak = jnp.max(scores, axis=1, keepdims=True)
            probs = jnp.exp(scores - peak)
            total = jnp.sum(probs, axis=1, keepdims=True)
            mixed = jnp.dot(probs.astype(jnp.bfloat16), vals, preferred_element_type=jnp.float32)
            hid[:, cols] = li[:, cols].astype(jnp.float32) + mixed / total

        step = 3 if per_part % 3 == 0 else 1

        @pl.loop(0, per_part // step)
        def _(i):
            for j in range(step):
                one_head(part * per_part + i * step + j)

    square = jnp.zeros((TILE, TILE), jnp.float32)
    for h in range(heads):
        piece = hid[:, h * TILE:(h + 1) * TILE]
        square = square + piece * piece
    inverse = lax.rsqrt(jnp.sum(square, axis=1, keepdims=True) / features + 1e-06)
    logits = jnp.zeros((TILE, TILE), jnp.float32)
    for h in range(heads):
        cols = slice(h * TILE, (h + 1) * TILE)
        piece = (hid[:, cols] * inverse * gain[:, cols]).astype(jnp.bfloat16)
        g[r, :, cols] = piece
        logits = logits + jnp.dot(piece, router[cols, :], preferred_element_type=jnp.float32)
    gates = jax.nn.sigmoid(logits) * sel[...]
    high = gates.astype(jnp.bfloat16)
    low = (gates - high.astype(jnp.float32)).astype(jnp.bfloat16)
    lane = lax.broadcasted_iota(jnp.int32, (TILE, TILE), 1)
    g[r, :, features:] = jnp.where(
        lane < TILE // 2, high.astype(jnp.float32), low.astype(jnp.float32)
    ).astype(jnp.bfloat16)

    def send(src, dst, send_sem, recv_sem, who):
        return pltpu.make_async_remote_copy(
            src_ref=src, dst_ref=dst, send_sem=send_sem, recv_sem=recv_sem,
            device_id=who, device_id_type=MESH,
        )

    def block_up(t):
        b = 2 * t + c
        return send(g.at[b], g.at[b], agu.at[t], agr.at[b], above)

    def block_down(t):
        b = 2 * t + c
        return send(g.at[b], g.at[b], agd.at[t], agr.at[b], below)

    def block_side(t):
        b = 2 * t + c
        return send(g.at[b], g.at[b], ags.at[t], agr.at[b], sibling)

    def block_arrival(b):
        return send(g.at[b], g.at[b], ags.at[0], agr.at[b], sibling)

    def part_side(t):
        return send(p.at[2 * t + 1 - c], sib.at[t], pss.at[t], psr.at[t], sibling)

    height = TILE // SUM_PARTS

    def sum_up(t, n):
        piece = pl.ds(n * height, height)
        return send(p.at[2 * t + c, piece], fd.at[t, piece], ups.at[t, n], upr.at[t, n], above)

    def sum_down(t, n):
        piece = pl.ds(n * height, height)
        return send(p.at[2 * t + c, piece], fu.at[t, piece], dns.at[t, n], dnr.at[t, n], below)

    def expert_pair(t):
        pair = pl.ds(2 * t, 2)

        @pl.loop(0, hmid.shape[1] // 256)
        def _(n):
            cols = pl.ds(pl.multiple_of(n * 256, 256), 256)
            tokens = g[pair, :, :features].reshape(2 * TILE, features)
            up = jnp.dot(tokens, wup[:, cols], preferred_element_type=jnp.float32)
            hmid[:, cols] = jax.nn.gelu(up, approximate=True).astype(jnp.bfloat16)

        gate_lanes = g[pair, :, features:].reshape(2 * TILE, TILE).astype(jnp.float32)
        lanes = lax.broadcasted_iota(jnp.int32, (2 * TILE, TILE), 1)
        mine = (lanes == z) | (lanes == z + TILE // 2)
        gate = jnp.sum(jnp.where(mine, gate_lanes, 0.0), axis=1, keepdims=True)

        @pl.loop(0, features // 256)
        def _(n):
            cols = pl.ds(pl.multiple_of(n * 256, 256), 256)
            down = jnp.dot(hmid[...], wdn[:, cols], preferred_element_type=jnp.float32)
            p[pair, :, cols] = (down * gate).astype(jnp.bfloat16).reshape(2, TILE, 256)

        part_side(t).start()

    def chain(s):
        up_to = s
        down_to = chips - 1 - s
        goes_up = z < up_to
        goes_down = z > down_to

        @pl.when(goes_up)
        def _():
            part_side_arrival(up_to)

        @pl.when(goes_down)
        def _():
            part_side_arrival(down_to)

        for n in range(SUM_PARTS):
            piece = pl.ds(n * height, height)

            @pl.when(goes_up)
            def _():
                own = p[2 * up_to + c, piece].astype(jnp.float32) + sib[up_to, piece].astype(jnp.float32)
                p[2 * up_to + c, piece] = own.astype(jnp.bfloat16)

                @pl.when(has_below)
                def _():
                    sum_up(up_to, n).wait_recv()
                    p[2 * up_to + c, piece] = (own + fd[up_to, piece].astype(jnp.float32)).astype(jnp.bfloat16)

                sum_up(up_to, n).start()

            @pl.when(goes_down)
            def _():
                own = p[2 * down_to + c, piece].astype(jnp.float32) + sib[down_to, piece].astype(jnp.float32)
                p[2 * down_to + c, piece] = own.astype(jnp.bfloat16)

                @pl.when(has_above)
                def _():
                    sum_down(down_to, n).wait_recv()
                    p[2 * down_to + c, piece] = (own + fu[down_to, piece].astype(jnp.float32)).astype(jnp.bfloat16)

                sum_down(down_to, n).start()

    def part_side_arrival(t):
        part_side(t).wait_recv()

    block_side(z).start()

    @pl.when(has_above)
    def _():
        block_up(z).start()

    @pl.when(has_below)
    def _():
        block_down(z).start()

    load_up.wait()
    load_dn.wait()
    block_arrival(2 * z + 1 - c).wait_recv()
    expert_pair(z)
    for s in range(1, chips):
        @pl.when(z >= s)
        def _():
            t = z - s
            block_arrival(2 * t + c).wait_recv()
            block_side(t).start()

            @pl.when(has_above)
            def _():
                block_up(t).start()

        @pl.when(z + s < chips)
        def _():
            t = z + s
            block_arrival(2 * t + c).wait_recv()
            block_side(t).start()

            @pl.when(has_below)
            def _():
                block_down(t).start()

        @pl.when(z >= s)
        def _():
            t = z - s
            block_arrival(2 * t + 1 - c).wait_recv()
            expert_pair(t)

        @pl.when(z + s < chips)
        def _():
            t = z + s
            block_arrival(2 * t + 1 - c).wait_recv()
            expert_pair(t)

        if s >= 2:
            chain(s - 1)
    chain(chips - 1)

    part_side_arrival(z)
    for n in range(SUM_PARTS):
        piece = pl.ds(n * height, height)
        hid[piece] = hid[piece] + (
            p[2 * z + c, piece].astype(jnp.float32) + sib[z, piece].astype(jnp.float32)
        )

        @pl.when(has_below)
        def _():
            sum_up(z, n).wait_recv()
            hid[piece] = hid[piece] + fd[z, piece].astype(jnp.float32)

        @pl.when(has_above)
        def _():
            sum_down(z, n).wait_recv()
            hid[piece] = hid[piece] + fu[z, piece].astype(jnp.float32)

        out[piece] = hid[piece].astype(jnp.bfloat16)

    for part in range(HALO_PARTS):
        for side in range(4):
            @pl.when(sides[side][0])
            def _():
                halo(side, part, 0).wait_send()
                halo(side, part, 1).wait_send()
    for t in range(chips):
        block_side(t).wait_send()
        part_side(t).wait_send()

        @pl.when((t <= z) & has_above)
        def _():
            block_up(t).wait_send()

        @pl.when((t >= z) & has_below)
        def _():
            block_down(t).wait_send()

        for n in range(SUM_PARTS):
            @pl.when(z < t)
            def _():
                sum_up(t, n).wait_send()

            @pl.when(z > t)
            def _():
                sum_down(t, n).wait_send()


def local(
    layer_input, queries, key_input, values, key_tiles, expert_ids, norm_gain, router, w_up, w_down
):
    frames = lax.axis_size("frame")
    rows = lax.axis_size("row")
    features = layer_input.shape[1]
    experts = router.shape[1]
    if rows > 8:
        return plain(
            layer_input, queries, key_input, values, key_tiles, expert_ids, norm_gain, router,
            w_up, w_down,
        )
    f = lax.axis_index("frame")
    r = lax.axis_index("row")
    tile = f * rows + r
    candidates = jnp.stack([tile, tile - rows, tile + rows, tile - 1, tile + 1])
    inside = jnp.stack([r >= 0, f >= 1, f < frames - 1, r >= 1, r < rows - 1])
    listed = inside & jnp.any(key_tiles[0][:, None] == candidates[None, :], axis=0)
    bias = jnp.repeat(jnp.where(listed, 0.0, -1e30).astype(jnp.float32), TILE)[None, :]
    half = TILE // 2
    padded = jnp.pad(router, ((0, 0), (0, half - experts)))
    padded = jnp.concatenate([padded, padded], axis=1)
    lanes = jnp.arange(TILE, dtype=jnp.int32) % half
    sel = jnp.any(expert_ids[:, :, None] == lanes[None, None, :], axis=1).astype(jnp.float32)
    hidden = w_up.shape[2]
    bf = jnp.bfloat16
    chips = rows // 2
    dma = pltpu.SemaphoreType.DMA
    vmem = pl.BlockSpec(memory_space=pltpu.VMEM)
    anywhere = pl.BlockSpec(memory_space=pl.ANY)
    return pl.pallas_call(
        functools.partial(fused_kernel, frames, rows, features // TILE),
        out_shape=jax.ShapeDtypeStruct((TILE, features), bf),
        in_specs=[vmem] * 8 + [anywhere] * 2,
        out_specs=vmem,
        scratch_shapes=[
            pltpu.VMEM((4, TILE, features), bf),
            pltpu.VMEM((4, TILE, features), bf),
            pltpu.VMEM((TILE, features), jnp.float32),
            pltpu.VMEM((rows, TILE, features + TILE), bf),
            pltpu.VMEM((rows, TILE, features), bf),
            pltpu.VMEM((chips, TILE, features), bf),
            pltpu.VMEM((chips, TILE, features), bf),
            pltpu.VMEM((chips, TILE, features), bf),
            pltpu.VMEM((2 * TILE, hidden), bf),
            pltpu.VMEM((features, hidden), bf),
            pltpu.VMEM((hidden, features), bf),
            dma((2,)),
            dma((4, HALO_PARTS, 2)),
            dma((4, HALO_PARTS, 2)),
            dma((chips,)),
            dma((chips,)),
            dma((chips,)),
            dma((rows,)),
            dma((chips,)),
            dma((chips,)),
            dma((chips, SUM_PARTS)),
            dma((chips, SUM_PARTS)),
            dma((chips, SUM_PARTS)),
            dma((chips, SUM_PARTS)),
        ],
        compiler_params=pltpu.CompilerParams(
            collective_id=0, has_side_effects=True, vmem_limit_bytes=60 * 2**20
        ),
    )(
        layer_input, queries, key_input, values, bias, norm_gain[None, :], padded, sel,
        w_up, w_down,
    )


def solution(mesh):
    return jax.shard_map(
        local,
        mesh=mesh,
        in_specs=(
            P(("groups", "frame", "row"), None),
            P(("groups", "frame", "row"), None),
            P(("groups", "frame", "row"), None),
            P(("groups", "frame", "row"), None),
            P(("groups", "frame", "row"), None),
            P(("groups", "frame", "row"), None),
            P(),
            P(),
            P("row", None, None),
            P("row", None, None),
        ),
        out_specs=P(("groups", "frame", "row"), None),
        check_vma=False,
    )
```

```python
import functools

import jax
import jax.numpy as jnp
from jax import lax
from jax.experimental import pallas as pl
from jax.experimental.pallas import tpu as pltpu
from jax.sharding import PartitionSpec as P

HEADS = 24
TILE = 128


def shifted(value, axis, steps):
    count = lax.axis_size(axis)
    initial, last = (max(0, -steps), min(count, count - steps))
    return lax.ppermute(value, axis, [(source, source + steps) for source in range(initial, last)])


def with_halo(block, sides, width):
    for axis, dim in sides:
        count = lax.axis_size(axis)
        forward = [(i, i + 1) for i in range(count - 1)]
        backward = [(target, source) for source, target in forward]
        low = lax.ppermute(
            lax.slice_in_dim(block, block.shape[dim] - width, None, axis=dim), axis, forward
        )
        high = lax.ppermute(lax.slice_in_dim(block, 0, width, axis=dim), axis, backward)
        block = jnp.concatenate([low, block, high], axis=dim)
    return block


def tile_partials(query_rows, key_rows, value_rows, head_count):
    batches, row_count, features = query_rows.shape
    head_size = features // head_count
    query_split = query_rows.reshape(batches, row_count, head_count, head_size)
    key_split = key_rows.reshape(batches, -1, head_count, head_size)
    value_split = value_rows.reshape(batches, -1, head_count, head_size)
    scores = jnp.einsum(
        "bqhd,bkhd->bhqk", query_split, key_split, preferred_element_type=jnp.float32
    ) * head_size ** (-0.5)
    maxima = jnp.max(scores, axis=-1)
    expos = jnp.exp(scores - maxima[..., None])
    totals = jnp.sum(expos, axis=-1)
    mixed = jnp.einsum(
        "bhqk,bkhd->bqhd",
        expos.astype(jnp.bfloat16),
        value_split,
        preferred_element_type=jnp.float32,
    )
    mixed = mixed / jnp.transpose(totals, (0, 2, 1))[..., None]
    return (mixed.reshape(batches, row_count, features).astype(jnp.bfloat16), maxima, totals)


def merge_partials(partial_value, maxima, totals, listed, head_count):
    masked = jnp.where(listed[:, :, None, None], maxima, -jnp.inf)
    peak_value = jnp.max(masked, axis=1, keepdims=True)
    weights = totals * jnp.exp(masked - peak_value)
    weight_sum = jnp.sum(weights, axis=1)
    tiles_here, cands, row_count, features = partial_value.shape
    split = partial_value.reshape(tiles_here, cands, row_count, head_count, features // head_count)
    scaled = jnp.sum(split * jnp.transpose(weights, (0, 1, 3, 2))[..., None], axis=1)
    merged = scaled / jnp.transpose(weight_sum, (0, 2, 1))[..., None]
    return merged.reshape(tiles_here, row_count, features)


def frame_return(part_out, part_max, part_sum, offset):
    return (
        shifted(part_out.astype(jnp.float32), "frame", offset).astype(part_out.dtype),
        shifted(part_max, "frame", offset),
        shifted(part_sum, "frame", offset),
    )


def row_return(part_out, part_max, part_sum, offset):
    return (
        shifted(part_out.astype(jnp.float32), "row", offset).astype(part_out.dtype),
        shifted(part_max, "row", offset),
        shifted(part_sum, "row", offset),
    )


def half_expert(token_rows, w_up, w_down):
    up_part = jnp.dot(token_rows, w_up[0], preferred_element_type=jnp.float32)
    inner = jax.nn.gelu(up_part, approximate=True).astype(jnp.bfloat16)
    return jnp.dot(inner, w_down[0], preferred_element_type=jnp.float32).astype(jnp.bfloat16)


def plain(
    layer_input, queries, key_input, values, key_tiles, expert_ids, norm_gain, router, w_up, w_down
):
    head_count = HEADS
    tile_rows = TILE
    per_device = key_tiles.shape[0]
    features = layer_input.shape[1]
    frame_index = lax.axis_index("frame")
    row_index = lax.axis_index("row")
    frame_count = lax.axis_size("frame")
    row_count = lax.axis_size("row")
    row_tiles = row_count * per_device
    query_tiles = queries.reshape(per_device, tile_rows, features)
    extended = with_halo(query_tiles[None], (("frame", 0), ("row", 1)), 1)
    middle = extended[1]
    visitors = jnp.stack(
        [
            query_tiles,
            extended[0, 1 : per_device + 1],
            extended[2, 1 : per_device + 1],
            middle[0:per_device],
            middle[2 : per_device + 2],
        ]
    )
    own_keys = jnp.broadcast_to(
        key_input.reshape(1, per_device, tile_rows, features), (5, per_device, tile_rows, features)
    )
    own_values = jnp.broadcast_to(
        values.reshape(1, per_device, tile_rows, features), (5, per_device, tile_rows, features)
    )
    flat_shape = (5 * per_device, tile_rows, features)
    partial_value, maxima, totals = tile_partials(
        visitors.reshape(flat_shape),
        own_keys.reshape(flat_shape),
        own_values.reshape(flat_shape),
        head_count,
    )
    partial_value = partial_value.reshape(5, per_device, tile_rows, features)
    maxima = maxima.reshape(5, per_device, head_count, tile_rows)
    totals = totals.reshape(5, per_device, head_count, tile_rows)
    from_lower = frame_return(partial_value[2], maxima[2], totals[2], 1)
    from_upper = frame_return(partial_value[1], maxima[1], totals[1], -1)
    below_edge = row_return(partial_value[4], maxima[4], totals[4], 1)
    above_edge = row_return(partial_value[3], maxima[3], totals[3], -1)
    local_sets = (partial_value, maxima, totals)
    from_below = tuple(
        (
            jnp.concatenate([below_edge[member], local_sets[member][4][: per_device - 1]], axis=0)
            for member in range(3)
        )
    )
    from_above = tuple(
        (
            jnp.concatenate([local_sets[member][3][1:], above_edge[member]], axis=0)
            for member in range(3)
        )
    )
    pieces = [
        (partial_value[0], maxima[0], totals[0]),
        from_lower,
        from_upper,
        from_below,
        from_above,
    ]
    partial_value = jnp.stack([piece[0].astype(jnp.float32) for piece in pieces], axis=1)
    maxima = jnp.stack([piece[1] for piece in pieces], axis=1)
    totals = jnp.stack([piece[2] for piece in pieces], axis=1)
    local_tiles = jnp.arange(per_device, dtype=jnp.int32)
    row_pos = row_index * per_device + local_tiles
    tile_id = frame_index * row_tiles + row_pos
    cand_ids = jnp.stack(
        [tile_id, tile_id - row_tiles, tile_id + row_tiles, tile_id - 1, tile_id + 1], axis=1
    )
    inside = jnp.stack(
        [
            jnp.ones((per_device,), bool),
            jnp.broadcast_to(frame_index >= 1, (per_device,)),
            jnp.broadcast_to(frame_index < frame_count - 1, (per_device,)),
            row_pos >= 1,
            row_pos < row_tiles - 1,
        ],
        axis=1,
    )
    listed = inside & jnp.any(key_tiles[:, :, None] == cand_ids[:, None, :], axis=1)
    attended = merge_partials(partial_value, maxima, totals, listed, head_count)
    hidden_state = layer_input.astype(jnp.float32) + attended.reshape(-1, features)
    mean_square = jnp.mean(hidden_state * hidden_state, axis=1, keepdims=True)
    normed = (hidden_state * lax.rsqrt(mean_square + 1e-06) * norm_gain).astype(jnp.bfloat16)
    logits = jnp.dot(normed, router, preferred_element_type=jnp.float32)
    token_count = normed.shape[0]
    expert_count = router.shape[1]
    capacity = min(token_count, max(2, 4 * token_count // expert_count))
    expert_range = jnp.arange(expert_count, dtype=jnp.int32)
    selector = expert_ids[:, :, None] == expert_range[None, None, :]
    gates = jax.nn.sigmoid(jnp.sum(logits[:, None, :] * selector.astype(jnp.float32), axis=2))
    onehot = selector.astype(jnp.int32).reshape(token_count * 2, expert_count)
    earlier = jnp.cumsum(onehot, axis=0) - onehot
    slot_index = jnp.sum(earlier * onehot, axis=1)
    flat_ids = expert_ids.reshape(-1)
    doubled = jnp.repeat(normed, 2, axis=0)
    outgoing = (
        jnp.zeros((expert_count, capacity, features), jnp.bfloat16)
        .at[flat_ids, slot_index]
        .set(doubled)
    )
    padded_out = jnp.repeat(outgoing, 2, axis=0)
    arrived = lax.all_to_all(padded_out, "row", split_axis=0, concat_axis=0, tiled=True)
    result = half_expert(arrived.reshape(-1, features), w_up, w_down)
    returned = lax.all_to_all(
        result.reshape(arrived.shape), "row", split_axis=0, concat_axis=0, tiled=True
    )
    halves = returned.reshape(expert_count, 2, capacity, features)
    both = halves[:, 0].astype(jnp.float32) + halves[:, 1].astype(jnp.float32)
    picked = both[flat_ids, slot_index].reshape(token_count, 2, features)
    return (hidden_state + jnp.sum(gates[:, :, None] * picked, axis=1)).astype(jnp.bfloat16)


HALO_PARTS = 6
SUM_PARTS = 4
MESH = pl.DeviceIdType.MESH


def fused_kernel(
    frames, rows, heads,
    li, q, k, v, bias, gain, router, sel, wup_hbm, wdn_hbm,
    out,
    kb, vb, hid, square, logits, g, p, sib, fd, fu, hmid, wup, wdn,
    wsem, hsend, hrecv, agu, agd, ags, agr, pss, psr, ups, dns, upr, dnr,
):
    chips = rows // 2
    features = q.shape[1]
    f = lax.axis_index("frame")
    r = lax.axis_index("row")
    z = r // 2
    c = r % 2
    sibling = {"row": 2 * z + 1 - c}
    above = {"row": r + 2}
    below = {"row": r - 2}
    has_above = z < chips - 1
    has_below = z > 0
    relayed = frames == 4
    first, last = f == 0, f == frames - 1
    sides = (
        (f > 0, {"frame": f - 1}, 1),
        (f < frames - 1, {"frame": f + 1}, 0),
        (r > 0, {"row": r - 1}, 3),
        (r < rows - 1, {"row": r + 1}, 2),
    )

    load_up = pltpu.make_async_copy(wup_hbm.at[0], wup, wsem.at[0])
    load_dn = pltpu.make_async_copy(wdn_hbm.at[0], wdn, wsem.at[1])
    load_up.start()
    load_dn.start()

    barrier = pltpu.get_barrier_semaphore()
    partners = sides + ((has_below, below, 0), (has_above, above, 0))
    if relayed:
        partners += ((f >= 0, {"frame": lax.rem(f + 2, 4)}, 0),)
    direct = [side[0] for side in sides]
    if relayed:
        direct[0] = direct[0] & (f != 2)
        direct[1] = direct[1] & (f != 1)
    for there, who, _ in partners:
        @pl.when(there)
        def _():
            pl.semaphore_signal(barrier, inc=1, device_id=who, device_id_type=MESH)
    peers = sum(jnp.where(there, 1, 0) for there, _, _ in partners)
    pl.semaphore_wait(barrier, peers)

    width = features // HALO_PARTS

    def halo(side, part, which):
        _, who, slot = sides[side]
        cols = pl.ds(part * width, width)
        src, dst = ((k, kb), (v, vb))[which]
        return pltpu.make_async_remote_copy(
            src_ref=src.at[:, cols],
            dst_ref=dst.at[slot, :, cols],
            send_sem=hsend.at[side, part, which],
            recv_sem=hrecv.at[slot, part, which],
            device_id=who,
            device_id_type=MESH,
        )

    def halo_arrival(slot, part, which):
        cols = pl.ds(part * width, width)
        src, dst = ((k, kb), (v, vb))[which]
        return pltpu.make_async_remote_copy(
            src_ref=src.at[:, cols],
            dst_ref=dst.at[slot, :, cols],
            send_sem=hsend.at[slot, part, which],
            recv_sem=hrecv.at[slot, part, which],
            device_id=sides[slot][1],
            device_id_type=MESH,
        )

    def relay(slot, part, which):
        cols = pl.ds(part * width, width)
        buffer = (kb, vb)[which]
        return pltpu.make_async_remote_copy(
            src_ref=buffer.at[1 - slot, :, cols],
            dst_ref=buffer.at[slot, :, cols],
            send_sem=hsend.at[slot, part, which],
            recv_sem=hrecv.at[slot, part, which],
            device_id={"frame": lax.rem(f + 2, 4)},
            device_id_type=MESH,
        )

    for part in range(HALO_PARTS):
        for side in range(4):
            @pl.when(direct[side])
            def _():
                halo(side, part, 0).start()
                halo(side, part, 1).start()
    for slot in range(4):
        @pl.when(jnp.logical_not(sides[slot][0]))
        def _():
            kb[slot] = jnp.zeros(kb.shape[1:], kb.dtype)
            vb[slot] = jnp.zeros(vb.shape[1:], vb.dtype)

    def send(src, dst, send_sem, recv_sem, who):
        return pltpu.make_async_remote_copy(
            src_ref=src, dst_ref=dst, send_sem=send_sem, recv_sem=recv_sem,
            device_id=who, device_id_type=MESH,
        )

    def stretch(b, part):
        if part == HALO_PARTS:
            return g.at[b, :, pl.ds(features, TILE)]
        return g.at[b, :, pl.ds(part * width, width)]

    def block_up(t, part):
        b = 2 * t + c
        return send(stretch(b, part), stretch(b, part), agu.at[t, part], agr.at[b, part], above)

    def block_down(t, part):
        b = 2 * t + c
        return send(stretch(b, part), stretch(b, part), agd.at[t, part], agr.at[b, part], below)

    def block_side(t, part):
        b = 2 * t + c
        return send(stretch(b, part), stretch(b, part), ags.at[t, part], agr.at[b, part], sibling)

    def block_arrival(b, part):
        return send(stretch(b, part), stretch(b, part), ags.at[0, part], agr.at[b, part], sibling)

    def gather(stage):
        if stage <= HALO_PARTS:
            @pl.when(has_above)
            def _():
                block_up(z, stage).start()

            @pl.when(has_below)
            def _():
                block_down(z, stage).start()

            block_side(z, stage).start()
        for d in range(1, chips):
            part = stage - d
            if part < 0 or part > HALO_PARTS:
                continue

            @pl.when(z >= d)
            def _():
                t = z - d
                block_arrival(2 * t + c, part).wait_recv()

                @pl.when(has_above)
                def _():
                    block_up(t, part).start()

                block_side(t, part).start()

            @pl.when(z + d < chips)
            def _():
                t = z + d
                block_arrival(2 * t + c, part).wait_recv()

                @pl.when(has_below)
                def _():
                    block_down(t, part).start()

                block_side(t, part).start()

    square[...] = jnp.zeros_like(square)
    logits[...] = jnp.zeros_like(logits)
    scale = TILE ** -0.5
    per_part = heads // HALO_PARTS
    for part in range(HALO_PARTS):
        for slot in range(4):
            @pl.when(sides[slot][0])
            def _():
                halo_arrival(slot, part, 0).wait_recv()
                halo_arrival(slot, part, 1).wait_recv()

            if relayed and slot < 2:
                @pl.when(last if slot == 0 else first)
                def _():
                    relay(1 - slot, part, 0).start()
                    relay(1 - slot, part, 1).start()

        def one_head(h):
            cols = pl.ds(pl.multiple_of(h * TILE, TILE), TILE)
            keys = jnp.concatenate([k[:, cols]] + [kb[s, :, cols] for s in range(4)], axis=0)
            vals = jnp.concatenate([v[:, cols]] + [vb[s, :, cols] for s in range(4)], axis=0)
            scores = lax.dot_general(
                q[:, cols], keys, (((1,), (1,)), ((), ())), preferred_element_type=jnp.float32
            ) * scale + bias[...]
            peak = jnp.max(scores, axis=1, keepdims=True)
            probs = jnp.exp(scores - peak)
            total = jnp.sum(probs, axis=1, keepdims=True)
            mixed = jnp.dot(probs.astype(jnp.bfloat16), vals, preferred_element_type=jnp.float32)
            state = li[:, cols].astype(jnp.float32) + mixed / total
            hid[:, cols] = state
            square[...] = square[...] + state * state
            token = (state * gain[:, cols]).astype(jnp.bfloat16)
            g[r, :, cols] = token
            logits[...] = logits[...] + jnp.dot(
                token, router[cols, :], preferred_element_type=jnp.float32
            )

        step = 2 if per_part % 2 == 0 else 1

        @pl.loop(0, per_part // step)
        def _(i):
            for j in range(step):
                one_head(part * per_part + i * step + j)

        gather(part)

    inverse = lax.rsqrt(jnp.sum(square[...], axis=1, keepdims=True) / features + 1e-06)
    gates = jax.nn.sigmoid(logits[...] * inverse) * sel[...]
    lane = lax.broadcasted_iota(jnp.int32, (TILE, TILE), 1)
    gates = jnp.where((lane == TILE // 4) | (lane == 3 * TILE // 4), inverse, gates)
    high = gates.astype(jnp.bfloat16)
    low = (gates - high.astype(jnp.float32)).astype(jnp.bfloat16)
    g[r, :, features:] = jnp.where(
        lane < TILE // 2, high.astype(jnp.float32), low.astype(jnp.float32)
    ).astype(jnp.bfloat16)

    for stage in range(HALO_PARTS, HALO_PARTS + chips):
        gather(stage)

    def part_side(t):
        return send(p.at[2 * t + 1 - c], sib.at[t], pss.at[t], psr.at[t], sibling)

    height = TILE // SUM_PARTS

    def sum_up(t, n):
        piece = pl.ds(n * height, height)
        return send(p.at[2 * t + c, piece], fd.at[t, piece], ups.at[t, n], upr.at[t, n], above)

    def sum_down(t, n):
        piece = pl.ds(n * height, height)
        return send(p.at[2 * t + c, piece], fu.at[t, piece], dns.at[t, n], dnr.at[t, n], below)

    def expert_pair(t):
        pair = pl.ds(2 * t, 2)
        tail = g[pair, :, features:].reshape(2 * TILE, TILE).astype(jnp.float32)
        lanes = lax.broadcasted_iota(jnp.int32, (2 * TILE, TILE), 1)
        mine = (lanes == z) | (lanes == z + TILE // 2)
        gate = jnp.sum(jnp.where(mine, tail, 0.0), axis=1, keepdims=True)
        norms = (lanes == TILE // 4) | (lanes == 3 * TILE // 4)
        inverse = jnp.sum(jnp.where(norms, tail, 0.0), axis=1, keepdims=True)

        @pl.loop(0, hmid.shape[1] // 256)
        def _(n):
            cols = pl.ds(pl.multiple_of(n * 256, 256), 256)
            tokens = g[pair, :, :features].reshape(2 * TILE, features)
            up = jnp.dot(tokens, wup[:, cols], preferred_element_type=jnp.float32)
            hmid[:, cols] = jax.nn.gelu(up * inverse, approximate=True).astype(jnp.bfloat16)

        @pl.loop(0, features // 256)
        def _(n):
            cols = pl.ds(pl.multiple_of(n * 256, 256), 256)
            down = jnp.dot(hmid[...], wdn[:, cols], preferred_element_type=jnp.float32)
            p[pair, :, cols] = (down * gate).astype(jnp.bfloat16).reshape(2, TILE, 256)

        part_side(t).start()

    def part_side_arrival(t):
        part_side(t).wait_recv()

    def pass_up(t, head):
        part_side_arrival(t)
        for n in range(SUM_PARTS):
            piece = pl.ds(n * height, height)
            total = p[2 * t + c, piece].astype(jnp.float32) + sib[t, piece].astype(jnp.float32)
            if not head:
                sum_up(t, n).wait_recv()
                total = total + fd[t, piece].astype(jnp.float32)
            p[2 * t + c, piece] = total.astype(jnp.bfloat16)
            sum_up(t, n).start()

    def pass_down(t, head):
        part_side_arrival(t)
        for n in range(SUM_PARTS):
            piece = pl.ds(n * height, height)
            total = p[2 * t + c, piece].astype(jnp.float32) + sib[t, piece].astype(jnp.float32)
            if not head:
                sum_down(t, n).wait_recv()
                total = total + fu[t, piece].astype(jnp.float32)
            p[2 * t + c, piece] = total.astype(jnp.bfloat16)
            sum_down(t, n).start()

    load_up.wait()
    load_dn.wait()
    for t in range(chips):
        for part in range(HALO_PARTS + 1):
            block_arrival(2 * t + 1 - c, part).wait_recv()

    for s in range(chips - 1, 0, -1):
        far = chips - 1 - s

        @pl.when(z < s)
        def _():
            expert_pair(s)

        @pl.when(z == 0)
        def _():
            pass_up(s, True)

        @pl.when(z > far)
        def _():
            expert_pair(far)

        @pl.when(z == chips - 1)
        def _():
            pass_down(far, True)

    expert_pair(z)
    for s in range(chips - 1, 0, -1):
        far = chips - 1 - s

        @pl.when((z < s) & has_below)
        def _():
            pass_up(s, False)

        @pl.when((z > far) & has_above)
        def _():
            pass_down(far, False)

    part_side_arrival(z)
    for n in range(SUM_PARTS):
        piece = pl.ds(n * height, height)
        hid[piece] = hid[piece] + (
            p[2 * z + c, piece].astype(jnp.float32) + sib[z, piece].astype(jnp.float32)
        )

        @pl.when(has_below)
        def _():
            sum_up(z, n).wait_recv()
            hid[piece] = hid[piece] + fd[z, piece].astype(jnp.float32)

        @pl.when(has_above)
        def _():
            sum_down(z, n).wait_recv()
            hid[piece] = hid[piece] + fu[z, piece].astype(jnp.float32)

        out[piece] = hid[piece].astype(jnp.bfloat16)

    for part in range(HALO_PARTS):
        for side in range(4):
            @pl.when(direct[side])
            def _():
                halo(side, part, 0).wait_send()
                halo(side, part, 1).wait_send()

        if relayed:
            @pl.when(first)
            def _():
                relay(0, part, 0).wait_send()
                relay(0, part, 1).wait_send()

            @pl.when(last)
            def _():
                relay(1, part, 0).wait_send()
                relay(1, part, 1).wait_send()
    for t in range(chips):
        part_side(t).wait_send()
        for part in range(HALO_PARTS + 1):
            block_side(t, part).wait_send()

            @pl.when((t <= z) & has_above)
            def _():
                block_up(t, part).wait_send()

            @pl.when((t >= z) & has_below)
            def _():
                block_down(t, part).wait_send()

        for n in range(SUM_PARTS):
            @pl.when(z < t)
            def _():
                sum_up(t, n).wait_send()

            @pl.when(z > t)
            def _():
                sum_down(t, n).wait_send()


def local(
    layer_input, queries, key_input, values, key_tiles, expert_ids, norm_gain, router, w_up, w_down
):
    frames = lax.axis_size("frame")
    rows = lax.axis_size("row")
    features = layer_input.shape[1]
    experts = router.shape[1]
    if rows > 8:
        return plain(
            layer_input, queries, key_input, values, key_tiles, expert_ids, norm_gain, router,
            w_up, w_down,
        )
    f = lax.axis_index("frame")
    r = lax.axis_index("row")
    tile = f * rows + r
    candidates = jnp.stack([tile, tile - rows, tile + rows, tile - 1, tile + 1])
    inside = jnp.stack([r >= 0, f >= 1, f < frames - 1, r >= 1, r < rows - 1])
    listed = inside & jnp.any(key_tiles[0][:, None] == candidates[None, :], axis=0)
    bias = jnp.repeat(jnp.where(listed, 0.0, -1e30).astype(jnp.float32), TILE)[None, :]
    half = TILE // 2
    padded = jnp.pad(router, ((0, 0), (0, half - experts)))
    padded = jnp.concatenate([padded, padded], axis=1)
    lanes = jnp.arange(TILE, dtype=jnp.int32) % half
    sel = jnp.any(expert_ids[:, :, None] == lanes[None, None, :], axis=1).astype(jnp.float32)
    hidden = w_up.shape[2]
    bf = jnp.bfloat16
    chips = rows // 2
    dma = pltpu.SemaphoreType.DMA
    vmem = pl.BlockSpec(memory_space=pltpu.VMEM)
    anywhere = pl.BlockSpec(memory_space=pl.ANY)
    return pl.pallas_call(
        functools.partial(fused_kernel, frames, rows, features // TILE),
        out_shape=jax.ShapeDtypeStruct((TILE, features), bf),
        in_specs=[vmem] * 8 + [anywhere] * 2,
        out_specs=vmem,
        scratch_shapes=[
            pltpu.VMEM((4, TILE, features), bf),
            pltpu.VMEM((4, TILE, features), bf),
            pltpu.VMEM((TILE, features), jnp.float32),
            pltpu.VMEM((TILE, TILE), jnp.float32),
            pltpu.VMEM((TILE, TILE), jnp.float32),
            pltpu.VMEM((rows, TILE, features + TILE), bf),
            pltpu.VMEM((rows, TILE, features), bf),
            pltpu.VMEM((chips, TILE, features), bf),
            pltpu.VMEM((chips, TILE, features), bf),
            pltpu.VMEM((chips, TILE, features), bf),
            pltpu.VMEM((2 * TILE, hidden), bf),
            pltpu.VMEM((features, hidden), bf),
            pltpu.VMEM((hidden, features), bf),
            dma((2,)),
            dma((4, HALO_PARTS, 2)),
            dma((4, HALO_PARTS, 2)),
            dma((chips, HALO_PARTS + 1)),
            dma((chips, HALO_PARTS + 1)),
            dma((chips, HALO_PARTS + 1)),
            dma((rows, HALO_PARTS + 1)),
            dma((chips,)),
            dma((chips,)),
            dma((chips, SUM_PARTS)),
            dma((chips, SUM_PARTS)),
            dma((chips, SUM_PARTS)),
            dma((chips, SUM_PARTS)),
        ],
        compiler_params=pltpu.CompilerParams(
            collective_id=0, has_side_effects=True, vmem_limit_bytes=60 * 2**20
        ),
    )(
        layer_input, queries, key_input, values, bias, norm_gain[None, :], padded, sel,
        w_up, w_down,
    )


def solution(mesh):
    return jax.shard_map(
        local,
        mesh=mesh,
        in_specs=(
            P(("groups", "frame", "row"), None),
            P(("groups", "frame", "row"), None),
            P(("groups", "frame", "row"), None),
            P(("groups", "frame", "row"), None),
            P(("groups", "frame", "row"), None),
            P(("groups", "frame", "row"), None),
            P(),
            P(),
            P("row", None, None),
            P("row", None, None),
        ),
        out_specs=P(("groups", "frame", "row"), None),
        check_vma=False,
    )
```

```python
import functools

import jax
import jax.numpy as jnp
from jax import lax
from jax.experimental import pallas as pl
from jax.experimental.pallas import tpu as pltpu
from jax.sharding import PartitionSpec as P

HEADS = 24
TILE = 128


def shifted(value, axis, steps):
    count = lax.axis_size(axis)
    initial, last = (max(0, -steps), min(count, count - steps))
    return lax.ppermute(value, axis, [(source, source + steps) for source in range(initial, last)])


def with_halo(block, sides, width):
    for axis, dim in sides:
        count = lax.axis_size(axis)
        forward = [(i, i + 1) for i in range(count - 1)]
        backward = [(target, source) for source, target in forward]
        low = lax.ppermute(
            lax.slice_in_dim(block, block.shape[dim] - width, None, axis=dim), axis, forward
        )
        high = lax.ppermute(lax.slice_in_dim(block, 0, width, axis=dim), axis, backward)
        block = jnp.concatenate([low, block, high], axis=dim)
    return block


def tile_partials(query_rows, key_rows, value_rows, head_count):
    batches, row_count, features = query_rows.shape
    head_size = features // head_count
    query_split = query_rows.reshape(batches, row_count, head_count, head_size)
    key_split = key_rows.reshape(batches, -1, head_count, head_size)
    value_split = value_rows.reshape(batches, -1, head_count, head_size)
    scores = jnp.einsum(
        "bqhd,bkhd->bhqk", query_split, key_split, preferred_element_type=jnp.float32
    ) * head_size ** (-0.5)
    maxima = jnp.max(scores, axis=-1)
    expos = jnp.exp(scores - maxima[..., None])
    totals = jnp.sum(expos, axis=-1)
    mixed = jnp.einsum(
        "bhqk,bkhd->bqhd",
        expos.astype(jnp.bfloat16),
        value_split,
        preferred_element_type=jnp.float32,
    )
    mixed = mixed / jnp.transpose(totals, (0, 2, 1))[..., None]
    return (mixed.reshape(batches, row_count, features).astype(jnp.bfloat16), maxima, totals)


def merge_partials(partial_value, maxima, totals, listed, head_count):
    masked = jnp.where(listed[:, :, None, None], maxima, -jnp.inf)
    peak_value = jnp.max(masked, axis=1, keepdims=True)
    weights = totals * jnp.exp(masked - peak_value)
    weight_sum = jnp.sum(weights, axis=1)
    tiles_here, cands, row_count, features = partial_value.shape
    split = partial_value.reshape(tiles_here, cands, row_count, head_count, features // head_count)
    scaled = jnp.sum(split * jnp.transpose(weights, (0, 1, 3, 2))[..., None], axis=1)
    merged = scaled / jnp.transpose(weight_sum, (0, 2, 1))[..., None]
    return merged.reshape(tiles_here, row_count, features)


def frame_return(part_out, part_max, part_sum, offset):
    return (
        shifted(part_out.astype(jnp.float32), "frame", offset).astype(part_out.dtype),
        shifted(part_max, "frame", offset),
        shifted(part_sum, "frame", offset),
    )


def row_return(part_out, part_max, part_sum, offset):
    return (
        shifted(part_out.astype(jnp.float32), "row", offset).astype(part_out.dtype),
        shifted(part_max, "row", offset),
        shifted(part_sum, "row", offset),
    )


def half_expert(token_rows, w_up, w_down):
    up_part = jnp.dot(token_rows, w_up[0], preferred_element_type=jnp.float32)
    inner = jax.nn.gelu(up_part, approximate=True).astype(jnp.bfloat16)
    return jnp.dot(inner, w_down[0], preferred_element_type=jnp.float32).astype(jnp.bfloat16)


def plain(
    layer_input, queries, key_input, values, key_tiles, expert_ids, norm_gain, router, w_up, w_down
):
    head_count = HEADS
    tile_rows = TILE
    per_device = key_tiles.shape[0]
    features = layer_input.shape[1]
    frame_index = lax.axis_index("frame")
    row_index = lax.axis_index("row")
    frame_count = lax.axis_size("frame")
    row_count = lax.axis_size("row")
    row_tiles = row_count * per_device
    query_tiles = queries.reshape(per_device, tile_rows, features)
    extended = with_halo(query_tiles[None], (("frame", 0), ("row", 1)), 1)
    middle = extended[1]
    visitors = jnp.stack(
        [
            query_tiles,
            extended[0, 1 : per_device + 1],
            extended[2, 1 : per_device + 1],
            middle[0:per_device],
            middle[2 : per_device + 2],
        ]
    )
    own_keys = jnp.broadcast_to(
        key_input.reshape(1, per_device, tile_rows, features), (5, per_device, tile_rows, features)
    )
    own_values = jnp.broadcast_to(
        values.reshape(1, per_device, tile_rows, features), (5, per_device, tile_rows, features)
    )
    flat_shape = (5 * per_device, tile_rows, features)
    partial_value, maxima, totals = tile_partials(
        visitors.reshape(flat_shape),
        own_keys.reshape(flat_shape),
        own_values.reshape(flat_shape),
        head_count,
    )
    partial_value = partial_value.reshape(5, per_device, tile_rows, features)
    maxima = maxima.reshape(5, per_device, head_count, tile_rows)
    totals = totals.reshape(5, per_device, head_count, tile_rows)
    from_lower = frame_return(partial_value[2], maxima[2], totals[2], 1)
    from_upper = frame_return(partial_value[1], maxima[1], totals[1], -1)
    below_edge = row_return(partial_value[4], maxima[4], totals[4], 1)
    above_edge = row_return(partial_value[3], maxima[3], totals[3], -1)
    local_sets = (partial_value, maxima, totals)
    from_below = tuple(
        (
            jnp.concatenate([below_edge[member], local_sets[member][4][: per_device - 1]], axis=0)
            for member in range(3)
        )
    )
    from_above = tuple(
        (
            jnp.concatenate([local_sets[member][3][1:], above_edge[member]], axis=0)
            for member in range(3)
        )
    )
    pieces = [
        (partial_value[0], maxima[0], totals[0]),
        from_lower,
        from_upper,
        from_below,
        from_above,
    ]
    partial_value = jnp.stack([piece[0].astype(jnp.float32) for piece in pieces], axis=1)
    maxima = jnp.stack([piece[1] for piece in pieces], axis=1)
    totals = jnp.stack([piece[2] for piece in pieces], axis=1)
    local_tiles = jnp.arange(per_device, dtype=jnp.int32)
    row_pos = row_index * per_device + local_tiles
    tile_id = frame_index * row_tiles + row_pos
    cand_ids = jnp.stack(
        [tile_id, tile_id - row_tiles, tile_id + row_tiles, tile_id - 1, tile_id + 1], axis=1
    )
    inside = jnp.stack(
        [
            jnp.ones((per_device,), bool),
            jnp.broadcast_to(frame_index >= 1, (per_device,)),
            jnp.broadcast_to(frame_index < frame_count - 1, (per_device,)),
            row_pos >= 1,
            row_pos < row_tiles - 1,
        ],
        axis=1,
    )
    listed = inside & jnp.any(key_tiles[:, :, None] == cand_ids[:, None, :], axis=1)
    attended = merge_partials(partial_value, maxima, totals, listed, head_count)
    hidden_state = layer_input.astype(jnp.float32) + attended.reshape(-1, features)
    mean_square = jnp.mean(hidden_state * hidden_state, axis=1, keepdims=True)
    normed = (hidden_state * lax.rsqrt(mean_square + 1e-06) * norm_gain).astype(jnp.bfloat16)
    logits = jnp.dot(normed, router, preferred_element_type=jnp.float32)
    token_count = normed.shape[0]
    expert_count = router.shape[1]
    capacity = min(token_count, max(2, 4 * token_count // expert_count))
    expert_range = jnp.arange(expert_count, dtype=jnp.int32)
    selector = expert_ids[:, :, None] == expert_range[None, None, :]
    gates = jax.nn.sigmoid(jnp.sum(logits[:, None, :] * selector.astype(jnp.float32), axis=2))
    onehot = selector.astype(jnp.int32).reshape(token_count * 2, expert_count)
    earlier = jnp.cumsum(onehot, axis=0) - onehot
    slot_index = jnp.sum(earlier * onehot, axis=1)
    flat_ids = expert_ids.reshape(-1)
    doubled = jnp.repeat(normed, 2, axis=0)
    outgoing = (
        jnp.zeros((expert_count, capacity, features), jnp.bfloat16)
        .at[flat_ids, slot_index]
        .set(doubled)
    )
    padded_out = jnp.repeat(outgoing, 2, axis=0)
    arrived = lax.all_to_all(padded_out, "row", split_axis=0, concat_axis=0, tiled=True)
    result = half_expert(arrived.reshape(-1, features), w_up, w_down)
    returned = lax.all_to_all(
        result.reshape(arrived.shape), "row", split_axis=0, concat_axis=0, tiled=True
    )
    halves = returned.reshape(expert_count, 2, capacity, features)
    both = halves[:, 0].astype(jnp.float32) + halves[:, 1].astype(jnp.float32)
    picked = both[flat_ids, slot_index].reshape(token_count, 2, features)
    return (hidden_state + jnp.sum(gates[:, :, None] * picked, axis=1)).astype(jnp.bfloat16)


HALO_PARTS = 6
SUM_PARTS = 4
LAG = 2
MESH = pl.DeviceIdType.MESH


def fused_kernel(
    frames, rows, heads,
    li, q, k, v, bias, gain, router, sel, wup_hbm, wdn_hbm,
    out,
    kb, vb, hid, square, logits, g, p, sib, fd, fu, hmid, wup, wdn,
    wsem, hsend, hrecv, agu, agd, ags, agr, pss, psr, ups, dns, upr, dnr,
):
    chips = rows // 2
    features = q.shape[1]
    f = lax.axis_index("frame")
    r = lax.axis_index("row")
    z = r // 2
    c = r % 2
    sibling = {"row": 2 * z + 1 - c}
    above = {"row": r + 2}
    below = {"row": r - 2}
    has_above = z < chips - 1
    has_below = z > 0
    relayed = frames == 4
    first, last = f == 0, f == frames - 1
    sides = (
        (f > 0, {"frame": f - 1}, 1),
        (f < frames - 1, {"frame": f + 1}, 0),
        (r > 0, {"row": r - 1}, 3),
        (r < rows - 1, {"row": r + 1}, 2),
    )

    load_up = pltpu.make_async_copy(wup_hbm.at[0], wup, wsem.at[0])
    load_dn = pltpu.make_async_copy(wdn_hbm.at[0], wdn, wsem.at[1])
    load_up.start()
    load_dn.start()

    barrier = pltpu.get_barrier_semaphore()
    partners = sides + ((has_below, below, 0), (has_above, above, 0))
    if relayed:
        partners += ((f >= 0, {"frame": lax.rem(f + 2, 4)}, 0),)
    direct = [side[0] for side in sides]
    if relayed:
        direct[0] = direct[0] & (f != 2)
        direct[1] = direct[1] & (f != 1)
    for there, who, _ in partners:
        @pl.when(there)
        def _():
            pl.semaphore_signal(barrier, inc=1, device_id=who, device_id_type=MESH)
    peers = sum(jnp.where(there, 1, 0) for there, _, _ in partners)
    pl.semaphore_wait(barrier, peers)

    width = features // HALO_PARTS

    def halo(side, part, which):
        _, who, slot = sides[side]
        cols = pl.ds(part * width, width)
        src, dst = ((k, kb), (v, vb))[which]
        return pltpu.make_async_remote_copy(
            src_ref=src.at[:, cols],
            dst_ref=dst.at[slot, :, cols],
            send_sem=hsend.at[side, part, which],
            recv_sem=hrecv.at[slot, part, which],
            device_id=who,
            device_id_type=MESH,
        )

    def halo_arrival(slot, part, which):
        cols = pl.ds(part * width, width)
        src, dst = ((k, kb), (v, vb))[which]
        return pltpu.make_async_remote_copy(
            src_ref=src.at[:, cols],
            dst_ref=dst.at[slot, :, cols],
            send_sem=hsend.at[slot, part, which],
            recv_sem=hrecv.at[slot, part, which],
            device_id=sides[slot][1],
            device_id_type=MESH,
        )

    def relay(slot, part, which):
        cols = pl.ds(part * width, width)
        buffer = (kb, vb)[which]
        return pltpu.make_async_remote_copy(
            src_ref=buffer.at[1 - slot, :, cols],
            dst_ref=buffer.at[slot, :, cols],
            send_sem=hsend.at[slot, part, which],
            recv_sem=hrecv.at[slot, part, which],
            device_id={"frame": lax.rem(f + 2, 4)},
            device_id_type=MESH,
        )

    for part in range(HALO_PARTS):
        for side in range(4):
            @pl.when(direct[side])
            def _():
                halo(side, part, 0).start()
                halo(side, part, 1).start()
    for slot in range(4):
        @pl.when(jnp.logical_not(sides[slot][0]))
        def _():
            kb[slot] = jnp.zeros(kb.shape[1:], kb.dtype)
            vb[slot] = jnp.zeros(vb.shape[1:], vb.dtype)

    def send(src, dst, send_sem, recv_sem, who):
        return pltpu.make_async_remote_copy(
            src_ref=src, dst_ref=dst, send_sem=send_sem, recv_sem=recv_sem,
            device_id=who, device_id_type=MESH,
        )

    def stretch(b, part):
        if part == HALO_PARTS:
            return g.at[b, :, pl.ds(features, TILE)]
        return g.at[b, :, pl.ds(part * width, width)]

    def block_up(t, part):
        b = 2 * t + c
        return send(stretch(b, part), stretch(b, part), agu.at[t, part], agr.at[b, part], above)

    def block_down(t, part):
        b = 2 * t + c
        return send(stretch(b, part), stretch(b, part), agd.at[t, part], agr.at[b, part], below)

    def block_side(t, part):
        b = 2 * t + c
        return send(stretch(b, part), stretch(b, part), ags.at[t, part], agr.at[b, part], sibling)

    def block_arrival(b, part):
        return send(stretch(b, part), stretch(b, part), ags.at[0, part], agr.at[b, part], sibling)

    def send_own(part):
        @pl.when(has_above)
        def _():
            block_up(z, part).start()

        @pl.when(has_below)
        def _():
            block_down(z, part).start()

        block_side(z, part).start()

    def forward(d, part):
        if d >= chips:
            return

        @pl.when(z >= d)
        def _():
            t = z - d
            block_arrival(2 * t + c, part).wait_recv()

            @pl.when(has_above)
            def _():
                block_up(t, part).start()

            block_side(t, part).start()

        @pl.when(z + d < chips)
        def _():
            t = z + d
            block_arrival(2 * t + c, part).wait_recv()

            @pl.when(has_below)
            def _():
                block_down(t, part).start()

            block_side(t, part).start()

    square[...] = jnp.zeros_like(square)
    logits[...] = jnp.zeros_like(logits)
    scale = TILE ** -0.5
    per_part = heads // HALO_PARTS
    for part in range(HALO_PARTS):
        for slot in range(4):
            @pl.when(sides[slot][0])
            def _():
                halo_arrival(slot, part, 0).wait_recv()
                halo_arrival(slot, part, 1).wait_recv()

            if relayed and slot < 2:
                @pl.when(last if slot == 0 else first)
                def _():
                    relay(1 - slot, part, 0).start()
                    relay(1 - slot, part, 1).start()

        def one_head(h):
            cols = pl.ds(pl.multiple_of(h * TILE, TILE), TILE)
            keys = jnp.concatenate([k[:, cols]] + [kb[s, :, cols] for s in range(4)], axis=0)
            vals = jnp.concatenate([v[:, cols]] + [vb[s, :, cols] for s in range(4)], axis=0)
            scores = lax.dot_general(
                q[:, cols], keys, (((1,), (1,)), ((), ())), preferred_element_type=jnp.float32
            ) * scale + bias[...]
            peak = jnp.max(scores, axis=1, keepdims=True)
            probs = jnp.exp(scores - peak)
            total = jnp.sum(probs, axis=1, keepdims=True)
            mixed = jnp.dot(probs.astype(jnp.bfloat16), vals, preferred_element_type=jnp.float32)
            state = li[:, cols].astype(jnp.float32) + mixed / total
            hid[:, cols] = state
            square[...] = square[...] + state * state
            token = (state * gain[:, cols]).astype(jnp.bfloat16)
            g[r, :, cols] = token
            logits[...] = logits[...] + jnp.dot(
                token, router[cols, :], preferred_element_type=jnp.float32
            )

        step = 2 if per_part % 2 == 0 else 1

        @pl.loop(0, per_part // step)
        def _(i):
            for j in range(step):
                one_head(part * per_part + i * step + j)

        send_own(part)
        if part >= LAG:
            forward(1, part - LAG)

    inverse = lax.rsqrt(jnp.sum(square[...], axis=1, keepdims=True) / features + 1e-06)
    gates = jax.nn.sigmoid(logits[...] * inverse) * sel[...]
    lane = lax.broadcasted_iota(jnp.int32, (TILE, TILE), 1)
    gates = jnp.where((lane == TILE // 4) | (lane == 3 * TILE // 4), inverse, gates)
    high = gates.astype(jnp.bfloat16)
    low = (gates - high.astype(jnp.float32)).astype(jnp.bfloat16)
    g[r, :, features:] = jnp.where(
        lane < TILE // 2, high.astype(jnp.float32), low.astype(jnp.float32)
    ).astype(jnp.bfloat16)

    send_own(HALO_PARTS)
    for part in range(HALO_PARTS - LAG, HALO_PARTS + 1):
        forward(1, part)
    for part in range(HALO_PARTS - LAG):
        forward(2, part)

    def part_side(t):
        return send(p.at[2 * t + 1 - c], sib.at[t], pss.at[t], psr.at[t], sibling)

    height = TILE // SUM_PARTS

    def sum_up(t, n):
        piece = pl.ds(n * height, height)
        return send(p.at[2 * t + c, piece], fd.at[t, piece], ups.at[t, n], upr.at[t, n], above)

    def sum_down(t, n):
        piece = pl.ds(n * height, height)
        return send(p.at[2 * t + c, piece], fu.at[t, piece], dns.at[t, n], dnr.at[t, n], below)

    def expert_pair(t):
        pair = pl.ds(2 * t, 2)
        tail = g[pair, :, features:].reshape(2 * TILE, TILE).astype(jnp.float32)
        lanes = lax.broadcasted_iota(jnp.int32, (2 * TILE, TILE), 1)
        mine = (lanes == z) | (lanes == z + TILE // 2)
        gate = jnp.sum(jnp.where(mine, tail, 0.0), axis=1, keepdims=True)
        norms = (lanes == TILE // 4) | (lanes == 3 * TILE // 4)
        inverse = jnp.sum(jnp.where(norms, tail, 0.0), axis=1, keepdims=True)

        @pl.loop(0, hmid.shape[1] // 256)
        def _(n):
            cols = pl.ds(pl.multiple_of(n * 256, 256), 256)
            tokens = g[pair, :, :features].reshape(2 * TILE, features)
            up = jnp.dot(tokens, wup[:, cols], preferred_element_type=jnp.float32)
            hmid[:, cols] = jax.nn.gelu(up * inverse, approximate=True).astype(jnp.bfloat16)

        @pl.loop(0, features // 256)
        def _(n):
            cols = pl.ds(pl.multiple_of(n * 256, 256), 256)
            down = jnp.dot(hmid[...], wdn[:, cols], preferred_element_type=jnp.float32)
            p[pair, :, cols] = (down * gate).astype(jnp.bfloat16).reshape(2, TILE, 256)

        part_side(t).start()

    def part_side_arrival(t):
        part_side(t).wait_recv()

    def pass_up(t, n, head):
        piece = pl.ds(n * height, height)
        total = p[2 * t + c, piece].astype(jnp.float32) + sib[t, piece].astype(jnp.float32)
        if not head:
            sum_up(t, n).wait_recv()
            total = total + fd[t, piece].astype(jnp.float32)
        p[2 * t + c, piece] = total.astype(jnp.bfloat16)
        sum_up(t, n).start()

    def pass_down(t, n, head):
        piece = pl.ds(n * height, height)
        total = p[2 * t + c, piece].astype(jnp.float32) + sib[t, piece].astype(jnp.float32)
        if not head:
            sum_down(t, n).wait_recv()
            total = total + fu[t, piece].astype(jnp.float32)
        p[2 * t + c, piece] = total.astype(jnp.bfloat16)
        sum_down(t, n).start()

    def experts_of(t):
        for part in range(HALO_PARTS + 1):
            block_arrival(2 * t + 1 - c, part).wait_recv()
        expert_pair(t)

    load_up.wait()
    load_dn.wait()
    experts_of(z)
    for part in range(HALO_PARTS - LAG, HALO_PARTS + 1):
        forward(2, part)
    for d in range(1, chips):
        @pl.when(z >= d)
        def _():
            experts_of(z - d)

            @pl.when(z == chips - 1)
            def _():
                part_side_arrival(chips - 1 - d)
                for n in range(SUM_PARTS):
                    pass_down(chips - 1 - d, n, True)

        @pl.when(z + d < chips)
        def _():
            experts_of(z + d)

            @pl.when(z == 0)
            def _():
                part_side_arrival(d)
                for n in range(SUM_PARTS):
                    pass_up(d, n, True)

        if d + 2 < chips:
            for part in range(HALO_PARTS + 1):
                forward(d + 2, part)

    for s in range(2, chips):
        far = chips - 1 - s
        goes_up = (z < s) & has_below
        goes_down = (z > far) & has_above

        @pl.when(goes_up)
        def _():
            part_side_arrival(s)

        @pl.when(goes_down)
        def _():
            part_side_arrival(far)

        for n in range(SUM_PARTS):
            @pl.when(goes_up)
            def _():
                pass_up(s, n, False)

            @pl.when(goes_down)
            def _():
                pass_down(far, n, False)

    part_side_arrival(z)
    for n in range(SUM_PARTS):
        piece = pl.ds(n * height, height)
        hid[piece] = hid[piece] + (
            p[2 * z + c, piece].astype(jnp.float32) + sib[z, piece].astype(jnp.float32)
        )

        @pl.when(has_below)
        def _():
            sum_up(z, n).wait_recv()
            hid[piece] = hid[piece] + fd[z, piece].astype(jnp.float32)

        @pl.when(has_above)
        def _():
            sum_down(z, n).wait_recv()
            hid[piece] = hid[piece] + fu[z, piece].astype(jnp.float32)

        out[piece] = hid[piece].astype(jnp.bfloat16)

    for part in range(HALO_PARTS):
        for side in range(4):
            @pl.when(direct[side])
            def _():
                halo(side, part, 0).wait_send()
                halo(side, part, 1).wait_send()

        if relayed:
            @pl.when(first)
            def _():
                relay(0, part, 0).wait_send()
                relay(0, part, 1).wait_send()

            @pl.when(last)
            def _():
                relay(1, part, 0).wait_send()
                relay(1, part, 1).wait_send()
    for t in range(chips):
        part_side(t).wait_send()
        for part in range(HALO_PARTS + 1):
            block_side(t, part).wait_send()

            @pl.when((t <= z) & has_above)
            def _():
                block_up(t, part).wait_send()

            @pl.when((t >= z) & has_below)
            def _():
                block_down(t, part).wait_send()

        for n in range(SUM_PARTS):
            @pl.when(z < t)
            def _():
                sum_up(t, n).wait_send()

            @pl.when(z > t)
            def _():
                sum_down(t, n).wait_send()


def local(
    layer_input, queries, key_input, values, key_tiles, expert_ids, norm_gain, router, w_up, w_down
):
    frames = lax.axis_size("frame")
    rows = lax.axis_size("row")
    features = layer_input.shape[1]
    experts = router.shape[1]
    if rows > 8:
        return plain(
            layer_input, queries, key_input, values, key_tiles, expert_ids, norm_gain, router,
            w_up, w_down,
        )
    f = lax.axis_index("frame")
    r = lax.axis_index("row")
    tile = f * rows + r
    candidates = jnp.stack([tile, tile - rows, tile + rows, tile - 1, tile + 1])
    inside = jnp.stack([r >= 0, f >= 1, f < frames - 1, r >= 1, r < rows - 1])
    listed = inside & jnp.any(key_tiles[0][:, None] == candidates[None, :], axis=0)
    bias = jnp.repeat(jnp.where(listed, 0.0, -1e30).astype(jnp.float32), TILE)[None, :]
    half = TILE // 2
    padded = jnp.pad(router, ((0, 0), (0, half - experts)))
    padded = jnp.concatenate([padded, padded], axis=1)
    lanes = jnp.arange(TILE, dtype=jnp.int32) % half
    sel = jnp.any(expert_ids[:, :, None] == lanes[None, None, :], axis=1).astype(jnp.float32)
    hidden = w_up.shape[2]
    bf = jnp.bfloat16
    chips = rows // 2
    dma = pltpu.SemaphoreType.DMA
    vmem = pl.BlockSpec(memory_space=pltpu.VMEM)
    anywhere = pl.BlockSpec(memory_space=pl.ANY)
    return pl.pallas_call(
        functools.partial(fused_kernel, frames, rows, features // TILE),
        out_shape=jax.ShapeDtypeStruct((TILE, features), bf),
        in_specs=[vmem] * 8 + [anywhere] * 2,
        out_specs=vmem,
        scratch_shapes=[
            pltpu.VMEM((4, TILE, features), bf),
            pltpu.VMEM((4, TILE, features), bf),
            pltpu.VMEM((TILE, features), jnp.float32),
            pltpu.VMEM((TILE, TILE), jnp.float32),
            pltpu.VMEM((TILE, TILE), jnp.float32),
            pltpu.VMEM((rows, TILE, features + TILE), bf),
            pltpu.VMEM((rows, TILE, features), bf),
            pltpu.VMEM((chips, TILE, features), bf),
            pltpu.VMEM((chips, TILE, features), bf),
            pltpu.VMEM((chips, TILE, features), bf),
            pltpu.VMEM((2 * TILE, hidden), bf),
            pltpu.VMEM((features, hidden), bf),
            pltpu.VMEM((hidden, features), bf),
            dma((2,)),
            dma((4, HALO_PARTS, 2)),
            dma((4, HALO_PARTS, 2)),
            dma((chips, HALO_PARTS + 1)),
            dma((chips, HALO_PARTS + 1)),
            dma((chips, HALO_PARTS + 1)),
            dma((rows, HALO_PARTS + 1)),
            dma((chips,)),
            dma((chips,)),
            dma((chips, SUM_PARTS)),
            dma((chips, SUM_PARTS)),
            dma((chips, SUM_PARTS)),
            dma((chips, SUM_PARTS)),
        ],
        compiler_params=pltpu.CompilerParams(
            collective_id=0, has_side_effects=True, vmem_limit_bytes=60 * 2**20
        ),
    )(
        layer_input, queries, key_input, values, bias, norm_gain[None, :], padded, sel,
        w_up, w_down,
    )


def solution(mesh):
    return jax.shard_map(
        local,
        mesh=mesh,
        in_specs=(
            P(("groups", "frame", "row"), None),
            P(("groups", "frame", "row"), None),
            P(("groups", "frame", "row"), None),
            P(("groups", "frame", "row"), None),
            P(("groups", "frame", "row"), None),
            P(("groups", "frame", "row"), None),
            P(),
            P(),
            P("row", None, None),
            P("row", None, None),
        ),
        out_specs=P(("groups", "frame", "row"), None),
        check_vma=False,
    )
```

```python
import functools

import jax
import jax.numpy as jnp
from jax import lax
from jax.experimental import pallas as pl
from jax.experimental.pallas import tpu as pltpu
from jax.sharding import PartitionSpec as P

HEADS = 24
TILE = 128


def shifted(value, axis, steps):
    count = lax.axis_size(axis)
    initial, last = (max(0, -steps), min(count, count - steps))
    return lax.ppermute(value, axis, [(source, source + steps) for source in range(initial, last)])


def with_halo(block, sides, width):
    for axis, dim in sides:
        count = lax.axis_size(axis)
        forward = [(i, i + 1) for i in range(count - 1)]
        backward = [(target, source) for source, target in forward]
        low = lax.ppermute(
            lax.slice_in_dim(block, block.shape[dim] - width, None, axis=dim), axis, forward
        )
        high = lax.ppermute(lax.slice_in_dim(block, 0, width, axis=dim), axis, backward)
        block = jnp.concatenate([low, block, high], axis=dim)
    return block


def tile_partials(query_rows, key_rows, value_rows, head_count):
    batches, row_count, features = query_rows.shape
    head_size = features // head_count
    query_split = query_rows.reshape(batches, row_count, head_count, head_size)
    key_split = key_rows.reshape(batches, -1, head_count, head_size)
    value_split = value_rows.reshape(batches, -1, head_count, head_size)
    scores = jnp.einsum(
        "bqhd,bkhd->bhqk", query_split, key_split, preferred_element_type=jnp.float32
    ) * head_size ** (-0.5)
    maxima = jnp.max(scores, axis=-1)
    expos = jnp.exp(scores - maxima[..., None])
    totals = jnp.sum(expos, axis=-1)
    mixed = jnp.einsum(
        "bhqk,bkhd->bqhd",
        expos.astype(jnp.bfloat16),
        value_split,
        preferred_element_type=jnp.float32,
    )
    mixed = mixed / jnp.transpose(totals, (0, 2, 1))[..., None]
    return (mixed.reshape(batches, row_count, features).astype(jnp.bfloat16), maxima, totals)


def merge_partials(partial_value, maxima, totals, listed, head_count):
    masked = jnp.where(listed[:, :, None, None], maxima, -jnp.inf)
    peak_value = jnp.max(masked, axis=1, keepdims=True)
    weights = totals * jnp.exp(masked - peak_value)
    weight_sum = jnp.sum(weights, axis=1)
    tiles_here, cands, row_count, features = partial_value.shape
    split = partial_value.reshape(tiles_here, cands, row_count, head_count, features // head_count)
    scaled = jnp.sum(split * jnp.transpose(weights, (0, 1, 3, 2))[..., None], axis=1)
    merged = scaled / jnp.transpose(weight_sum, (0, 2, 1))[..., None]
    return merged.reshape(tiles_here, row_count, features)


def frame_return(part_out, part_max, part_sum, offset):
    return (
        shifted(part_out.astype(jnp.float32), "frame", offset).astype(part_out.dtype),
        shifted(part_max, "frame", offset),
        shifted(part_sum, "frame", offset),
    )


def row_return(part_out, part_max, part_sum, offset):
    return (
        shifted(part_out.astype(jnp.float32), "row", offset).astype(part_out.dtype),
        shifted(part_max, "row", offset),
        shifted(part_sum, "row", offset),
    )


def half_expert(token_rows, w_up, w_down):
    up_part = jnp.dot(token_rows, w_up[0], preferred_element_type=jnp.float32)
    inner = jax.nn.gelu(up_part, approximate=True).astype(jnp.bfloat16)
    return jnp.dot(inner, w_down[0], preferred_element_type=jnp.float32).astype(jnp.bfloat16)


def plain(
    layer_input, queries, key_input, values, key_tiles, expert_ids, norm_gain, router, w_up, w_down
):
    head_count = HEADS
    tile_rows = TILE
    per_device = key_tiles.shape[0]
    features = layer_input.shape[1]
    frame_index = lax.axis_index("frame")
    row_index = lax.axis_index("row")
    frame_count = lax.axis_size("frame")
    row_count = lax.axis_size("row")
    row_tiles = row_count * per_device
    query_tiles = queries.reshape(per_device, tile_rows, features)
    extended = with_halo(query_tiles[None], (("frame", 0), ("row", 1)), 1)
    middle = extended[1]
    visitors = jnp.stack(
        [
            query_tiles,
            extended[0, 1 : per_device + 1],
            extended[2, 1 : per_device + 1],
            middle[0:per_device],
            middle[2 : per_device + 2],
        ]
    )
    own_keys = jnp.broadcast_to(
        key_input.reshape(1, per_device, tile_rows, features), (5, per_device, tile_rows, features)
    )
    own_values = jnp.broadcast_to(
        values.reshape(1, per_device, tile_rows, features), (5, per_device, tile_rows, features)
    )
    flat_shape = (5 * per_device, tile_rows, features)
    partial_value, maxima, totals = tile_partials(
        visitors.reshape(flat_shape),
        own_keys.reshape(flat_shape),
        own_values.reshape(flat_shape),
        head_count,
    )
    partial_value = partial_value.reshape(5, per_device, tile_rows, features)
    maxima = maxima.reshape(5, per_device, head_count, tile_rows)
    totals = totals.reshape(5, per_device, head_count, tile_rows)
    from_lower = frame_return(partial_value[2], maxima[2], totals[2], 1)
    from_upper = frame_return(partial_value[1], maxima[1], totals[1], -1)
    below_edge = row_return(partial_value[4], maxima[4], totals[4], 1)
    above_edge = row_return(partial_value[3], maxima[3], totals[3], -1)
    local_sets = (partial_value, maxima, totals)
    from_below = tuple(
        (
            jnp.concatenate([below_edge[member], local_sets[member][4][: per_device - 1]], axis=0)
            for member in range(3)
        )
    )
    from_above = tuple(
        (
            jnp.concatenate([local_sets[member][3][1:], above_edge[member]], axis=0)
            for member in range(3)
        )
    )
    pieces = [
        (partial_value[0], maxima[0], totals[0]),
        from_lower,
        from_upper,
        from_below,
        from_above,
    ]
    partial_value = jnp.stack([piece[0].astype(jnp.float32) for piece in pieces], axis=1)
    maxima = jnp.stack([piece[1] for piece in pieces], axis=1)
    totals = jnp.stack([piece[2] for piece in pieces], axis=1)
    local_tiles = jnp.arange(per_device, dtype=jnp.int32)
    row_pos = row_index * per_device + local_tiles
    tile_id = frame_index * row_tiles + row_pos
    cand_ids = jnp.stack(
        [tile_id, tile_id - row_tiles, tile_id + row_tiles, tile_id - 1, tile_id + 1], axis=1
    )
    inside = jnp.stack(
        [
            jnp.ones((per_device,), bool),
            jnp.broadcast_to(frame_index >= 1, (per_device,)),
            jnp.broadcast_to(frame_index < frame_count - 1, (per_device,)),
            row_pos >= 1,
            row_pos < row_tiles - 1,
        ],
        axis=1,
    )
    listed = inside & jnp.any(key_tiles[:, :, None] == cand_ids[:, None, :], axis=1)
    attended = merge_partials(partial_value, maxima, totals, listed, head_count)
    hidden_state = layer_input.astype(jnp.float32) + attended.reshape(-1, features)
    mean_square = jnp.mean(hidden_state * hidden_state, axis=1, keepdims=True)
    normed = (hidden_state * lax.rsqrt(mean_square + 1e-06) * norm_gain).astype(jnp.bfloat16)
    logits = jnp.dot(normed, router, preferred_element_type=jnp.float32)
    token_count = normed.shape[0]
    expert_count = router.shape[1]
    capacity = min(token_count, max(2, 4 * token_count // expert_count))
    expert_range = jnp.arange(expert_count, dtype=jnp.int32)
    selector = expert_ids[:, :, None] == expert_range[None, None, :]
    gates = jax.nn.sigmoid(jnp.sum(logits[:, None, :] * selector.astype(jnp.float32), axis=2))
    onehot = selector.astype(jnp.int32).reshape(token_count * 2, expert_count)
    earlier = jnp.cumsum(onehot, axis=0) - onehot
    slot_index = jnp.sum(earlier * onehot, axis=1)
    flat_ids = expert_ids.reshape(-1)
    doubled = jnp.repeat(normed, 2, axis=0)
    outgoing = (
        jnp.zeros((expert_count, capacity, features), jnp.bfloat16)
        .at[flat_ids, slot_index]
        .set(doubled)
    )
    padded_out = jnp.repeat(outgoing, 2, axis=0)
    arrived = lax.all_to_all(padded_out, "row", split_axis=0, concat_axis=0, tiled=True)
    result = half_expert(arrived.reshape(-1, features), w_up, w_down)
    returned = lax.all_to_all(
        result.reshape(arrived.shape), "row", split_axis=0, concat_axis=0, tiled=True
    )
    halves = returned.reshape(expert_count, 2, capacity, features)
    both = halves[:, 0].astype(jnp.float32) + halves[:, 1].astype(jnp.float32)
    picked = both[flat_ids, slot_index].reshape(token_count, 2, features)
    return (hidden_state + jnp.sum(gates[:, :, None] * picked, axis=1)).astype(jnp.bfloat16)


HALO_PARTS = 6
SUM_PARTS = 8
MESH = pl.DeviceIdType.MESH


def fused_kernel(
    frames, rows, heads,
    li, q, k, v, bias, gain, router, sel, wup_hbm, wdn_hbm,
    out,
    kb, vb, hid, square, logits, g, p, sib, fd, fu, hmid, wup, wdn,
    wsem, hsend, hrecv, agu, agd, ags, agr, pss, psr, ups, dns, upr, dnr,
):
    chips = rows // 2
    features = q.shape[1]
    f = lax.axis_index("frame")
    r = lax.axis_index("row")
    z = r // 2
    c = r % 2
    sibling = {"row": 2 * z + 1 - c}
    above = {"row": r + 2}
    below = {"row": r - 2}
    has_above = z < chips - 1
    has_below = z > 0
    relayed = frames == 4
    first, last = f == 0, f == frames - 1
    sides = (
        (f > 0, {"frame": f - 1}, 1),
        (f < frames - 1, {"frame": f + 1}, 0),
        (r > 0, {"row": r - 1}, 3),
        (r < rows - 1, {"row": r + 1}, 2),
    )

    load_up = pltpu.make_async_copy(wup_hbm.at[0], wup, wsem.at[0])
    load_dn = pltpu.make_async_copy(wdn_hbm.at[0], wdn, wsem.at[1])
    load_up.start()
    load_dn.start()

    barrier = pltpu.get_barrier_semaphore()
    partners = sides + ((has_below, below, 0), (has_above, above, 0))
    if relayed:
        partners += ((f >= 0, {"frame": lax.rem(f + 2, 4)}, 0),)
    direct = [side[0] for side in sides]
    if relayed:
        direct[0] = direct[0] & (f != 2)
        direct[1] = direct[1] & (f != 1)
    for there, who, _ in partners:
        @pl.when(there)
        def _():
            pl.semaphore_signal(barrier, inc=1, device_id=who, device_id_type=MESH)
    peers = sum(jnp.where(there, 1, 0) for there, _, _ in partners)
    pl.semaphore_wait(barrier, peers)

    width = features // HALO_PARTS

    def halo(side, part, which):
        _, who, slot = sides[side]
        cols = pl.ds(part * width, width)
        src, dst = ((k, kb), (v, vb))[which]
        return pltpu.make_async_remote_copy(
            src_ref=src.at[:, cols],
            dst_ref=dst.at[slot, :, cols],
            send_sem=hsend.at[side, part, which],
            recv_sem=hrecv.at[slot, part, which],
            device_id=who,
            device_id_type=MESH,
        )

    def halo_arrival(slot, part, which):
        cols = pl.ds(part * width, width)
        src, dst = ((k, kb), (v, vb))[which]
        return pltpu.make_async_remote_copy(
            src_ref=src.at[:, cols],
            dst_ref=dst.at[slot, :, cols],
            send_sem=hsend.at[slot, part, which],
            recv_sem=hrecv.at[slot, part, which],
            device_id=sides[slot][1],
            device_id_type=MESH,
        )

    def relay(slot, part, which):
        cols = pl.ds(part * width, width)
        buffer = (kb, vb)[which]
        return pltpu.make_async_remote_copy(
            src_ref=buffer.at[1 - slot, :, cols],
            dst_ref=buffer.at[slot, :, cols],
            send_sem=hsend.at[slot, part, which],
            recv_sem=hrecv.at[slot, part, which],
            device_id={"frame": lax.rem(f + 2, 4)},
            device_id_type=MESH,
        )

    for part in range(HALO_PARTS):
        for side in range(4):
            @pl.when(direct[side])
            def _():
                halo(side, part, 0).start()
                halo(side, part, 1).start()
    for slot in range(4):
        @pl.when(jnp.logical_not(sides[slot][0]))
        def _():
            kb[slot] = jnp.zeros(kb.shape[1:], kb.dtype)
            vb[slot] = jnp.zeros(vb.shape[1:], vb.dtype)

    def send(src, dst, send_sem, recv_sem, who):
        return pltpu.make_async_remote_copy(
            src_ref=src, dst_ref=dst, send_sem=send_sem, recv_sem=recv_sem,
            device_id=who, device_id_type=MESH,
        )

    def stretch(b, part):
        if part == HALO_PARTS:
            return g.at[b, :, pl.ds(features, TILE)]
        return g.at[b, :, pl.ds(part * width, width)]

    def block_up(t, part):
        b = 2 * t + c
        return send(stretch(b, part), stretch(b, part), agu.at[t, part], agr.at[b, part], above)

    def block_down(t, part):
        b = 2 * t + c
        return send(stretch(b, part), stretch(b, part), agd.at[t, part], agr.at[b, part], below)

    def block_side(t, part):
        b = 2 * t + c
        return send(stretch(b, part), stretch(b, part), ags.at[t, part], agr.at[b, part], sibling)

    def block_arrival(b, part):
        return send(stretch(b, part), stretch(b, part), ags.at[0, part], agr.at[b, part], sibling)

    def gather(stage):
        if stage <= HALO_PARTS:
            @pl.when(has_above)
            def _():
                block_up(z, stage).start()

            @pl.when(has_below)
            def _():
                block_down(z, stage).start()

            block_side(z, stage).start()
        for d in range(1, chips):
            part = stage - d
            if part < 0 or part > HALO_PARTS:
                continue

            @pl.when(z >= d)
            def _():
                t = z - d
                block_arrival(2 * t + c, part).wait_recv()

                @pl.when(has_above)
                def _():
                    block_up(t, part).start()

                block_side(t, part).start()

            @pl.when(z + d < chips)
            def _():
                t = z + d
                block_arrival(2 * t + c, part).wait_recv()

                @pl.when(has_below)
                def _():
                    block_down(t, part).start()

                block_side(t, part).start()

    square[...] = jnp.zeros_like(square)
    logits[...] = jnp.zeros_like(logits)
    scale = TILE ** -0.5
    per_part = heads // HALO_PARTS
    for part in range(HALO_PARTS):
        for slot in range(4):
            @pl.when(sides[slot][0])
            def _():
                halo_arrival(slot, part, 0).wait_recv()
                halo_arrival(slot, part, 1).wait_recv()

            if relayed and slot < 2:
                @pl.when(last if slot == 0 else first)
                def _():
                    relay(1 - slot, part, 0).start()
                    relay(1 - slot, part, 1).start()

        def one_head(h):
            cols = pl.ds(pl.multiple_of(h * TILE, TILE), TILE)
            keys = jnp.concatenate([k[:, cols]] + [kb[s, :, cols] for s in range(4)], axis=0)
            vals = jnp.concatenate([v[:, cols]] + [vb[s, :, cols] for s in range(4)], axis=0)
            scores = lax.dot_general(
                q[:, cols], keys, (((1,), (1,)), ((), ())), preferred_element_type=jnp.float32
            ) * scale + bias[...]
            peak = jnp.max(scores, axis=1, keepdims=True)
            probs = jnp.exp(scores - peak)
            total = jnp.sum(probs, axis=1, keepdims=True)
            mixed = jnp.dot(probs.astype(jnp.bfloat16), vals, preferred_element_type=jnp.float32)
            state = li[:, cols].astype(jnp.float32) + mixed / total
            hid[:, cols] = state
            square[...] = square[...] + state * state
            token = (state * gain[:, cols]).astype(jnp.bfloat16)
            g[r, :, cols] = token
            logits[...] = logits[...] + jnp.dot(
                token, router[cols, :], preferred_element_type=jnp.float32
            )

        step = 2 if per_part % 2 == 0 else 1

        @pl.loop(0, per_part // step)
        def _(i):
            for j in range(step):
                one_head(part * per_part + i * step + j)

        gather(part)

    inverse = lax.rsqrt(jnp.sum(square[...], axis=1, keepdims=True) / features + 1e-06)
    gates = jax.nn.sigmoid(logits[...] * inverse) * sel[...]
    lane = lax.broadcasted_iota(jnp.int32, (TILE, TILE), 1)
    gates = jnp.where((lane == TILE // 4) | (lane == 3 * TILE // 4), inverse, gates)
    high = gates.astype(jnp.bfloat16)
    low = (gates - high.astype(jnp.float32)).astype(jnp.bfloat16)
    g[r, :, features:] = jnp.where(
        lane < TILE // 2, high.astype(jnp.float32), low.astype(jnp.float32)
    ).astype(jnp.bfloat16)

    for stage in range(HALO_PARTS, HALO_PARTS + chips):
        gather(stage)

    def part_side(t):
        return send(p.at[2 * t + 1 - c], sib.at[t], pss.at[t], psr.at[t], sibling)

    height = TILE // SUM_PARTS

    def sum_up(t, n):
        piece = pl.ds(n * height, height)
        return send(p.at[2 * t + c, piece], fd.at[t, piece], ups.at[t, n], upr.at[t, n], above)

    def sum_down(t, n):
        piece = pl.ds(n * height, height)
        return send(p.at[2 * t + c, piece], fu.at[t, piece], dns.at[t, n], dnr.at[t, n], below)

    def expert_pair(t):
        pair = pl.ds(2 * t, 2)
        tail = g[pair, :, features:].reshape(2 * TILE, TILE).astype(jnp.float32)
        lanes = lax.broadcasted_iota(jnp.int32, (2 * TILE, TILE), 1)
        mine = (lanes == z) | (lanes == z + TILE // 2)
        gate = jnp.sum(jnp.where(mine, tail, 0.0), axis=1, keepdims=True)
        norms = (lanes == TILE // 4) | (lanes == 3 * TILE // 4)
        inverse = jnp.sum(jnp.where(norms, tail, 0.0), axis=1, keepdims=True)

        @pl.loop(0, hmid.shape[1] // 256)
        def _(n):
            cols = pl.ds(pl.multiple_of(n * 256, 256), 256)
            tokens = g[pair, :, :features].reshape(2 * TILE, features)
            up = jnp.dot(tokens, wup[:, cols], preferred_element_type=jnp.float32)
            hmid[:, cols] = jax.nn.gelu(up * inverse, approximate=True).astype(jnp.bfloat16)

        @pl.loop(0, features // 256)
        def _(n):
            cols = pl.ds(pl.multiple_of(n * 256, 256), 256)
            down = jnp.dot(hmid[...], wdn[:, cols], preferred_element_type=jnp.float32)
            p[pair, :, cols] = (down * gate).astype(jnp.bfloat16).reshape(2, TILE, 256)

        part_side(t).start()

    def part_side_arrival(t):
        part_side(t).wait_recv()

    def pass_up(t, n, head):
        piece = pl.ds(n * height, height)
        total = p[2 * t + c, piece].astype(jnp.float32) + sib[t, piece].astype(jnp.float32)
        if not head:
            sum_up(t, n).wait_recv()
            total = total + fd[t, piece].astype(jnp.float32)
        p[2 * t + c, piece] = total.astype(jnp.bfloat16)
        sum_up(t, n).start()

    def pass_down(t, n, head):
        piece = pl.ds(n * height, height)
        total = p[2 * t + c, piece].astype(jnp.float32) + sib[t, piece].astype(jnp.float32)
        if not head:
            sum_down(t, n).wait_recv()
            total = total + fu[t, piece].astype(jnp.float32)
        p[2 * t + c, piece] = total.astype(jnp.bfloat16)
        sum_down(t, n).start()

    load_up.wait()
    load_dn.wait()
    for t in range(chips):
        for part in range(HALO_PARTS + 1):
            block_arrival(2 * t + 1 - c, part).wait_recv()

    for s in range(chips - 1, 0, -1):
        far = chips - 1 - s

        @pl.when(z < s)
        def _():
            expert_pair(s)

        @pl.when(z == 0)
        def _():
            part_side_arrival(s)
            for n in range(SUM_PARTS):
                pass_up(s, n, True)

        @pl.when(z > far)
        def _():
            expert_pair(far)

        @pl.when(z == chips - 1)
        def _():
            part_side_arrival(far)
            for n in range(SUM_PARTS):
                pass_down(far, n, True)

    expert_pair(z)
    for s in range(chips - 1, 1, -1):
        far = chips - 1 - s
        goes_up = (z < s) & has_below
        goes_down = (z > far) & has_above

        @pl.when(goes_up)
        def _():
            part_side_arrival(s)

        @pl.when(goes_down)
        def _():
            part_side_arrival(far)

        for n in range(SUM_PARTS):
            @pl.when(goes_up)
            def _():
                pass_up(s, n, False)

            @pl.when(goes_down)
            def _():
                pass_down(far, n, False)

    part_side_arrival(z)
    for n in range(SUM_PARTS):
        piece = pl.ds(n * height, height)
        hid[piece] = hid[piece] + (
            p[2 * z + c, piece].astype(jnp.float32) + sib[z, piece].astype(jnp.float32)
        )

        @pl.when(has_below)
        def _():
            sum_up(z, n).wait_recv()
            hid[piece] = hid[piece] + fd[z, piece].astype(jnp.float32)

        @pl.when(has_above)
        def _():
            sum_down(z, n).wait_recv()
            hid[piece] = hid[piece] + fu[z, piece].astype(jnp.float32)

        out[piece] = hid[piece].astype(jnp.bfloat16)

    for part in range(HALO_PARTS):
        for side in range(4):
            @pl.when(direct[side])
            def _():
                halo(side, part, 0).wait_send()
                halo(side, part, 1).wait_send()

        if relayed:
            @pl.when(first)
            def _():
                relay(0, part, 0).wait_send()
                relay(0, part, 1).wait_send()

            @pl.when(last)
            def _():
                relay(1, part, 0).wait_send()
                relay(1, part, 1).wait_send()
    for t in range(chips):
        part_side(t).wait_send()
        for part in range(HALO_PARTS + 1):
            block_side(t, part).wait_send()

            @pl.when((t <= z) & has_above)
            def _():
                block_up(t, part).wait_send()

            @pl.when((t >= z) & has_below)
            def _():
                block_down(t, part).wait_send()

        for n in range(SUM_PARTS):
            @pl.when(z < t)
            def _():
                sum_up(t, n).wait_send()

            @pl.when(z > t)
            def _():
                sum_down(t, n).wait_send()


def local(
    layer_input, queries, key_input, values, key_tiles, expert_ids, norm_gain, router, w_up, w_down
):
    frames = lax.axis_size("frame")
    rows = lax.axis_size("row")
    features = layer_input.shape[1]
    experts = router.shape[1]
    if rows > 8:
        return plain(
            layer_input, queries, key_input, values, key_tiles, expert_ids, norm_gain, router,
            w_up, w_down,
        )
    f = lax.axis_index("frame")
    r = lax.axis_index("row")
    tile = f * rows + r
    candidates = jnp.stack([tile, tile - rows, tile + rows, tile - 1, tile + 1])
    inside = jnp.stack([r >= 0, f >= 1, f < frames - 1, r >= 1, r < rows - 1])
    listed = inside & jnp.any(key_tiles[0][:, None] == candidates[None, :], axis=0)
    bias = jnp.repeat(jnp.where(listed, 0.0, -1e30).astype(jnp.float32), TILE)[None, :]
    half = TILE // 2
    padded = jnp.pad(router, ((0, 0), (0, half - experts)))
    padded = jnp.concatenate([padded, padded], axis=1)
    lanes = jnp.arange(TILE, dtype=jnp.int32) % half
    sel = jnp.any(expert_ids[:, :, None] == lanes[None, None, :], axis=1).astype(jnp.float32)
    hidden = w_up.shape[2]
    bf = jnp.bfloat16
    chips = rows // 2
    dma = pltpu.SemaphoreType.DMA
    vmem = pl.BlockSpec(memory_space=pltpu.VMEM)
    anywhere = pl.BlockSpec(memory_space=pl.ANY)
    return pl.pallas_call(
        functools.partial(fused_kernel, frames, rows, features // TILE),
        out_shape=jax.ShapeDtypeStruct((TILE, features), bf),
        in_specs=[vmem] * 8 + [anywhere] * 2,
        out_specs=vmem,
        scratch_shapes=[
            pltpu.VMEM((4, TILE, features), bf),
            pltpu.VMEM((4, TILE, features), bf),
            pltpu.VMEM((TILE, features), jnp.float32),
            pltpu.VMEM((TILE, TILE), jnp.float32),
            pltpu.VMEM((TILE, TILE), jnp.float32),
            pltpu.VMEM((rows, TILE, features + TILE), bf),
            pltpu.VMEM((rows, TILE, features), bf),
            pltpu.VMEM((chips, TILE, features), bf),
            pltpu.VMEM((chips, TILE, features), bf),
            pltpu.VMEM((chips, TILE, features), bf),
            pltpu.VMEM((2 * TILE, hidden), bf),
            pltpu.VMEM((features, hidden), bf),
            pltpu.VMEM((hidden, features), bf),
            dma((2,)),
            dma((4, HALO_PARTS, 2)),
            dma((4, HALO_PARTS, 2)),
            dma((chips, HALO_PARTS + 1)),
            dma((chips, HALO_PARTS + 1)),
            dma((chips, HALO_PARTS + 1)),
            dma((rows, HALO_PARTS + 1)),
            dma((chips,)),
            dma((chips,)),
            dma((chips, SUM_PARTS)),
            dma((chips, SUM_PARTS)),
            dma((chips, SUM_PARTS)),
            dma((chips, SUM_PARTS)),
        ],
        compiler_params=pltpu.CompilerParams(
            collective_id=0, has_side_effects=True, vmem_limit_bytes=60 * 2**20
        ),
    )(
        layer_input, queries, key_input, values, bias, norm_gain[None, :], padded, sel,
        w_up, w_down,
    )


def solution(mesh):
    return jax.shard_map(
        local,
        mesh=mesh,
        in_specs=(
            P(("groups", "frame", "row"), None),
            P(("groups", "frame", "row"), None),
            P(("groups", "frame", "row"), None),
            P(("groups", "frame", "row"), None),
            P(("groups", "frame", "row"), None),
            P(("groups", "frame", "row"), None),
            P(),
            P(),
            P("row", None, None),
            P("row", None, None),
        ),
        out_specs=P(("groups", "frame", "row"), None),
        check_vma=False,
    )
```
